32 devices in a mesh: fsdp: 16 (over z, y, core), rep: 2 (over x).
Axes of the slice: x: 2, y: 2, z: 4, core: 2. Of those that a mesh axis runs over, the one named last changes fastest.
Arguments:
- inputs: bfloat16 [8192, 1536], P(('fsdp', 'rep')), may hold values from -6 to 6
- segment_ids: int32 [32, 256], P(('fsdp', 'rep')), may hold values from 0 to 5, never falling along the last dimension, each value on 1 to 128 neighbouring positions
- norm_one: bfloat16 [1536], P(('fsdp', 'rep')), may hold values from 0.5 to 1.5
- w_query: bfloat16 [1536, 1536], P(('fsdp', 'rep')), may hold values from -0.15625 to 0.15625
- w_key: bfloat16 [1536, 1536], P(('fsdp', 'rep')), may hold values from -0.15625 to 0.15625
- w_value: bfloat16 [1536, 1536], P(('fsdp', 'rep')), may hold values from -0.15625 to 0.15625
- w_gate_out: bfloat16 [1536, 1536], P(('fsdp', 'rep')), may hold values from -0.15625 to 0.15625
- w_forget: bfloat16 [1536, 24], P(('fsdp', 'rep')), may hold values from -0.15625 to 0.15625
- forget_bias: bfloat16 [24], replicated, may hold values from 1 to 7
- w_output: bfloat16 [1536, 1536], P(('fsdp', 'rep')), may hold values from -0.625 to 0.625
- norm_two: bfloat16 [1536], P(('fsdp', 'rep')), may hold values from 0.5 to 1.5
- w_ffn_gate: bfloat16 [1536, 4096], P(('fsdp', 'rep')), may hold values from -0.15625 to 0.15625
- w_ffn_up: bfloat16 [1536, 4096], P(('fsdp', 'rep')), may hold values from -0.15625 to 0.15625
- w_ffn_down: bfloat16 [4096, 1536], P(('fsdp', 'rep')), may hold values from -0.09375 to 0.09375
- out_grad: bfloat16 [8192, 1536], P(('fsdp', 'rep')), may hold values from -6 to 6
Outputs:
- layer_output: bfloat16 [8192, 1536], P(('fsdp', 'rep'))
- input_grad: float32 [8192, 1536], P(('fsdp', 'rep'))
- norm_one_grad: float32 [1536], P(('fsdp', 'rep'))
- query_grad: float32 [1536, 1536], P(('fsdp', 'rep'))
- key_grad: float32 [1536, 1536], P(('fsdp', 'rep'))
- value_grad: float32 [1536, 1536], P(('fsdp', 'rep'))
- gate_out_grad: float32 [1536, 1536], P(('fsdp', 'rep'))
- forget_grad: float32 [1536, 24], P(('fsdp', 'rep'))
- forget_bias_grad: float32 [24], replicated
- w_output_grad: float32 [1536, 1536], P(('fsdp', 'rep'))
- norm_two_grad: float32 [1536], P(('fsdp', 'rep'))
- ffn_gate_grad: float32 [1536, 4096], P(('fsdp', 'rep'))
- ffn_up_grad: float32 [1536, 4096], P(('fsdp', 'rep'))
- ffn_down_grad: float32 [4096, 1536], P(('fsdp', 'rep'))
The draws below stay inside these ranges and needn't reach their ends.
Inputs may be any that keep to these rules, and one draw needn't show every extreme that they name: `segment_ids`: segment numbers never fall along a sequence; each document spans 1 to 128 tokens, and one spans exactly 128.
All inputs are finite; a program needn't handle non-finite values.
Results may differ from the reference program's by a relative error of at most 0.014.
Values may be sent and summed in bfloat16 or wider, within the bound.
No kernel may reach another device: no remote copies, remote signals or barrier semaphores. Data moves between devices by JAX's collectives and lax.ppermute only.
A program may use at most 384 MiB of HBM per device.

```python
import math
import jax
import jax.numpy as jnp
import numpy as np
from jax import lax

D = 1536
H = 24
HEAD = 64
FF = 4096
SEQ = 256
SEQS = 32
TOKENS = 8192


def levels(stream_key, shape, split, low, largest):
    level, own = 1.0, jax.random.fold_in(stream_key, 6)
    for axis_at, parts in split:
        heights = jnp.exp(jax.random.uniform(jax.random.fold_in(own, axis_at), (parts,), jnp.float32, low / len(split), largest / len(split)))
        level = level * jnp.repeat(heights, shape[axis_at] // parts).reshape([-1 if axis == axis_at else 1 for axis in range(len(shape))])
    return level


def profile(amount, total, limit, skew):
    loads = [(1 << 20) // math.isqrt(rank ** skew) + 1 for rank in range(2, amount + 1)]
    spare, counts = total - limit - (amount - 1), [1] * (amount - 1)
    while spare > 0:
        candidates = [i for i in range(amount - 1) if counts[i] < limit]
        pool, budget = sum([loads[i] for i in candidates]), spare
        for i in candidates:
            extra = min(limit - counts[i], max(1, budget * loads[i] // pool), spare)
            counts[i] = counts[i] + extra
            spare = spare - extra
    return np.array([limit] + counts)


def uneven_parts(rng, number_of, total, bound, lean):
    if number_of == 2:
        one = jax.random.randint(rng, (), max(1, total - bound), min(bound, total - 1) + 1)
        return jnp.stack([one, total - one])
    sizes = jnp.asarray(profile(number_of, total, bound, lean), jnp.int32)
    pairs = (number_of - 1) // 2
    source_of, taker = sizes[1:1 + 2 * pairs:2], sizes[2:2 + 2 * pairs:2]
    margin = jnp.minimum(source_of - 1, bound - taker)
    moved = jax.random.randint(jax.random.fold_in(rng, 1), (pairs,), 0, 1 << 20) % (margin + 1)
    sizes = sizes.at[1:1 + 2 * pairs:2].set(source_of - moved).at[2:2 + 2 * pairs:2].set(taker + moved)
    return sizes[jax.random.permutation(jax.random.fold_in(rng, 2), number_of)]


def noise(rng, dims, width, most, shards=(), dtype=jnp.bfloat16):
    loudness = levels(rng, dims, shards, -0.22, 0.18) if shards else 1.0
    array = jax.random.normal(rng, dims, jnp.float32) * width * loudness
    return jnp.minimum(jnp.maximum(array, -most), most).astype(dtype)


def setup_inputs(seed: int = 0) -> dict:
    key_list = jax.random.split(jax.random.key(seed), 16)
    return {
        "inputs": noise(key_list[0], (TOKENS, D), 1.0, 6.0, ((0, 32),)),
        "segment_ids": jax.vmap(lambda own: jnp.searchsorted(jnp.cumsum(uneven_parts(own, 6, SEQ, SEQ // 2, 1)), jnp.arange(SEQ), side="right"))(jax.random.split(key_list[1], SEQS)).reshape((SEQS, SEQ)).astype(jnp.int32),
        "norm_one": jnp.clip(1.0 + 0.1 * jax.random.normal(key_list[2], (D,), jnp.float32), 0.5, 1.5).astype(jnp.bfloat16),
        "w_query": noise(key_list[3], (D, D), D ** -0.5, 0.15625, ((0, 32),)),
        "w_key": noise(key_list[4], (D, D), D ** -0.5, 0.15625, ((0, 32),)),
        "w_value": noise(key_list[5], (D, D), D ** -0.5, 0.15625, ((0, 32),)),
        "w_gate_out": noise(key_list[6], (D, D), D ** -0.5, 0.15625, ((0, 32),)),
        "w_forget": noise(key_list[7], (D, H), D ** -0.5, 0.15625, ((0, 32),)),
        "forget_bias": jnp.clip(jax.random.uniform(key_list[8], (H,), jnp.float32, 1.0, 7.0), 1.0, 7.0).astype(jnp.bfloat16),
        "w_output": noise(key_list[9], (D, D), (D // 16) ** -0.5, 0.625, ((0, 32),)),
        "norm_two": jnp.clip(1.0 + 0.1 * jax.random.normal(key_list[10], (D,), jnp.float32), 0.5, 1.5).astype(jnp.bfloat16),
        "w_ffn_gate": noise(key_list[11], (D, FF), D ** -0.5, 0.15625, ((0, 32),)),
        "w_ffn_up": noise(key_list[12], (D, FF), D ** -0.5, 0.15625, ((0, 32),)),
        "w_ffn_down": noise(key_list[13], (FF, D), FF ** -0.5, 0.09375, ((0, 32),)),
        "out_grad": noise(key_list[14], (TOKENS, D), 1.0, 6.0, ((0, 32),)),
    }


epsilon = 1e-06
negative_big = -1e+30
highest = lax.Precision.HIGHEST

@jax.custom_vjp
def low(v):
    return lax.optimization_barrier(v.astype(jnp.bfloat16)).astype(jnp.float32)

@jax.custom_vjp
def low_back(v):
    return v

def low_keep(v):
    return (low(v), None)

def low_pass(kept, grad):
    return (grad,)

def back_keep(v):
    return (v, None)

def back_low(kept, grad):
    return (low(grad),)
low.defvjp(low_keep, low_pass)
low_back.defvjp(back_keep, back_low)

def product(left, right):
    return jnp.dot(left, right, precision=highest)

def heads_first(matrix):
    return matrix.reshape(SEQ, H, HEAD).transpose(1, 0, 2)

def layer(tokens, segment, gain_one, w_query, w_key, w_value, w_gate_out, w_forget, forget_bias, w_output, gain_two, w_ffn_gate, w_ffn_up, w_ffn_down):
    inv_one = lax.rsqrt(lax.optimization_barrier(jnp.mean(tokens * tokens, -1, keepdims=True)) + epsilon)
    normed = tokens * inv_one
    hidden_one = low(normed * gain_one)
    query_rows = low_back(low(product(hidden_one, w_query)))
    key_rows = low_back(low(product(hidden_one, w_key)))
    value_rows = low_back(low(product(hidden_one, w_value)))
    gate_pre = low_back(product(hidden_one, w_gate_out))
    out_gate = jax.nn.sigmoid(gate_pre)
    forget_pre = low_back(product(hidden_one, w_forget) + forget_bias)
    decay_sum = jnp.cumsum(jax.nn.log_sigmoid(forget_pre), axis=0).T
    scores = jnp.einsum('hid,hjd->hij', heads_first(query_rows), heads_first(key_rows), precision=highest) * 0.125
    scores = scores + decay_sum[:, :, None] - decay_sum[:, None, :]
    places = jnp.arange(SEQ)
    allowed = (segment[:, None] == segment[None, :]) & (places[None, :] <= places[:, None])
    scores = low_back(jnp.where(allowed[None], scores, negative_big))
    shifted = jnp.exp(scores - lax.optimization_barrier(jnp.max(scores, -1, keepdims=True)))
    att_probs = shifted / lax.optimization_barrier(jnp.sum(shifted, -1, keepdims=True))
    attended = low_back(jnp.einsum('hij,hjd->hid', low(att_probs), heads_first(value_rows), precision=highest))
    attended = attended.transpose(1, 0, 2).reshape(SEQ, D)
    gated_att = low(attended * out_gate)
    middle = tokens + low_back(product(gated_att, w_output))
    inv_two = lax.rsqrt(lax.optimization_barrier(jnp.mean(middle * middle, -1, keepdims=True)) + epsilon)
    hidden_two = low(middle * inv_two * gain_two)
    gate_ffn = low_back(product(hidden_two, w_ffn_gate))
    up_ffn = low_back(product(hidden_two, w_ffn_up))
    activation = low(jax.nn.silu(gate_ffn) * up_ffn)
    return middle + low_back(product(activation, w_ffn_down))

def reference(inputs, segment_ids, norm_one, w_query, w_key, w_value, w_gate_out, w_forget, forget_bias, w_output, norm_two, w_ffn_gate, w_ffn_up, w_ffn_down, out_grad):
    weights = tuple((weight.astype(jnp.float32) for weight in (norm_one, w_query, w_key, w_value, w_gate_out, w_forget, forget_bias, w_output, norm_two, w_ffn_gate, w_ffn_up, w_ffn_down)))

    def whole_layer(tokens, *params):

        def advance(running, seq_item):
            return (running, jax.checkpoint(layer)(seq_item[0], seq_item[1], *params))
        unused, result = lax.scan(advance, jnp.zeros((), jnp.float32), (tokens.reshape(SEQS, SEQ, D), segment_ids))
        return result.reshape(TOKENS, D)
    primal, pullback = jax.vjp(whole_layer, inputs.astype(jnp.float32), *weights)
    gradients = pullback(out_grad.astype(jnp.float32))
    return (primal.astype(jnp.bfloat16), gradients[0], gradients[1], gradients[2], gradients[3], gradients[4], gradients[5], gradients[6], gradients[7], gradients[8], gradients[9], gradients[10], gradients[11], gradients[12])
```

```python
import math

import jax
import jax.numpy as jnp
from jax import lax
from jax.experimental import pallas as pl
from jax.experimental.pallas import tpu as pltpu
from jax.sharding import Mesh
from jax.sharding import PartitionSpec as P

H = 24
HEAD = 64
Z = 4
GROUP = 4
LANES = 128
TILE = 256
LOCAL_HEADS = H // GROUP

epsilon = 1e-06
negative_big = -1e30
bf16 = jnp.bfloat16
f32 = jnp.float32
ALL = ("z", "w", "y", "c", "r", "x")
REST = ("w", "r")
ANY = pl.BlockSpec(memory_space=pl.ANY)
kernel_params = pltpu.CompilerParams(vmem_limit_bytes=48 * 1024 * 1024)


def row_norm(tokens):
    inverse_rms = lax.rsqrt(jnp.mean(tokens * tokens, -1, keepdims=True) + epsilon)
    return (tokens * inverse_rms, inverse_rms)


def norm_back(grad_hat, normed, inverse_rms):
    return inverse_rms * (grad_hat - normed * jnp.mean(grad_hat * normed, -1, keepdims=True))


def product(left, right):
    return jnp.dot(left, right, preferred_element_type=f32)


def product_nt(left, right, precision=None):
    return lax.dot_general(
        left, right, (((1,), (1,)), ((), ())), preferred_element_type=f32, precision=precision
    )


def product_tn(left, right, precision=None):
    return lax.dot_general(
        left, right, (((0,), (0,)), ((), ())), preferred_element_type=f32, precision=precision
    )


def place_in_ring(index):
    return index ^ (index >> 1)


def found_at(step):
    return place_in_ring((place_in_ring(lax.axis_index("z")) - step) & 3)


def along_z(block):
    return lax.ppermute(block, "z", [(0, 1), (1, 3), (3, 2), (2, 0)])


def swap(value, axis):
    return lax.ppermute(value, axis, [(0, 1), (1, 0)])


def has_rest():
    return lax.axis_size("w") * lax.axis_size("r") > 1


def over_rest(block):
    if not has_rest():
        return block[None, None]
    return lax.all_gather(lax.all_gather(block, "r"), "w")


def sum_over_rest(total):
    if not has_rest():
        return total[0, 0]
    return lax.psum_scatter(lax.psum_scatter(total, "w"), "r")


def order(values, after):
    count = len(values)
    if has_rest():
        return values
    return pl.pallas_call(
        lambda *refs: None,
        in_specs=[ANY] * (count + len(after)),
        out_specs=[ANY] * count,
        out_shape=[jax.ShapeDtypeStruct(value.shape, value.dtype) for value in values],
        input_output_aliases={at: at for at in range(count)},
        name="order",
    )(*values, *after)


def halves(part, axis):
    mine = lax.axis_index(axis)
    return [
        (part(found_at(step), 1 - mine), lambda step=step: part(found_at(step), mine).astype(f32))
        for step in range(1, Z + 1)
    ]


def arrange(arrivals, axis, shape, reorder, spots):
    mine = lax.axis_index(axis)
    blocks = [block for _, _, block in arrivals]
    if has_rest():
        whole = jnp.zeros((Z, 2, *blocks[0].shape), blocks[0].dtype)
        for step, other, block in arrivals:
            at = (found_at(step), mine ^ other)
            whole = lax.dynamic_update_slice(whole, block[None, None], (*at, *[0] * block.ndim))
        return reorder(whole)
    blocks = [block.reshape(-1, block.shape[-1]) for block in blocks]
    places = jnp.stack([found_at(step) for step in range(Z)] + [mine, 1 - mine]).astype(jnp.int32)

    def kernel(places_ref, *refs):
        block_refs, outs, sems = refs[: len(blocks)], refs[len(blocks) : -1], refs[-1]
        copies = []
        for at, (step, other, _) in enumerate(arrivals):
            for out, first, rows, spot in spots(outs, places_ref[step], places_ref[Z + other]):
                source = block_refs[at].at[pl.ds(first, rows)]
                copies.append(pltpu.make_async_copy(source, spot, sems.at[len(copies)]))
        for copy in copies:
            copy.start()
        for copy in copies:
            copy.wait()

    return pl.pallas_call(
        kernel,
        in_specs=[pl.BlockSpec(memory_space=pltpu.SMEM)]
        + [pl.BlockSpec(memory_space=pltpu.VMEM)] * len(blocks),
        out_specs=[ANY] * len(shape),
        out_shape=[jax.ShapeDtypeStruct(one, bf16) for one in shape],
        scratch_shapes=[pltpu.SemaphoreType.DMA((8 * len(blocks),))],
        compiler_params=kernel_params,
        name="arrange",
    )(places, *blocks)


def group_gather(own, axis):
    over = swap(own, axis)
    return jnp.concatenate((own, over, swap(own, "c"), swap(over, "c")), 0)


def group_scatter(partial, axis):
    rows = partial.shape[0] // GROUP
    from_core = swap(partial[2 * rows :], "c").astype(f32)
    near = partial[: 2 * rows].astype(f32) + from_core
    return near[:rows] + swap(near[rows:].astype(bf16), axis).astype(f32)


def exchange(shares, axes):
    return lax.all_to_all(shares, axes, 0, 0, tiled=True)


def transpose_quarters(block):
    return lax.ppermute(
        block, ("z", "c", "x"), [(i * GROUP + j, j * GROUP + i) for i in range(Z) for j in range(GROUP)]
    )


def pack_heads(weights):
    rows, width = weights[0].shape
    part = width // GROUP

    def kernel(*refs):
        for at, ref in enumerate(refs[:-1]):
            for to in range(GROUP):
                refs[-1][to, :, at * part : (at + 1) * part] = ref[:, to * part : (to + 1) * part]

    return pl.pallas_call(
        kernel, out_shape=jax.ShapeDtypeStruct((GROUP, rows, len(weights) * part), bf16), name="pack_heads"
    )(*weights)


def unpack_heads(shares, count):
    rows, part = shares.shape[1], shares.shape[2] // count

    def kernel(ref, *outs):
        for at, out in enumerate(outs):
            for to in range(GROUP):
                out[:, to * part : (to + 1) * part] = ref[to, :, at * part : (at + 1) * part].astype(f32)

    whole = jax.ShapeDtypeStruct((rows, GROUP * part), f32)
    return pl.pallas_call(kernel, out_shape=[whole] * count, name="unpack_heads")(shares)


def unit_chunks(unit):
    for at_z in range(Z):
        for place in range(GROUP):
            for at_x in range(2):
                here = (at_z * 2 + at_x) * unit
                yield place, here // TILE * 2 * TILE + here % TILE, ((at_z * GROUP + place) * 2 + at_x) * unit


def pack_units(gate, up, unit):
    rows, hidden = gate.shape
    part = hidden // GROUP
    if has_rest():
        size = (rows, Z, lax.axis_size("w"), 2, 2, lax.axis_size("r"), 2, unit)
        both = [
            one.reshape(size).transpose(3, 4, 0, 1, 6, 2, 5, 7).reshape(GROUP, rows, part // TILE, TILE)
            for one in (gate, up)
        ]
        return jnp.stack(both, 3).reshape(GROUP, rows, 2 * part)

    def kernel(gate_ref, up_ref, out):
        for place, here, there in unit_chunks(unit):
            out[place, :, here : here + unit] = gate_ref[:, there : there + unit]
            out[place, :, here + TILE : here + TILE + unit] = up_ref[:, there : there + unit]

    return pl.pallas_call(
        kernel, out_shape=jax.ShapeDtypeStruct((GROUP, rows, 2 * part), bf16), name="pack_units"
    )(gate, up)


def unpack_units(shares, unit):
    rows, part = shares.shape[1], shares.shape[2] // 2
    if has_rest():
        size = (2, 2, rows, Z, 2, lax.axis_size("w"), lax.axis_size("r"), unit)
        both = shares.reshape(GROUP, rows, part // TILE, 2, TILE)
        return [
            both[:, :, :, at].reshape(size).transpose(2, 3, 5, 0, 1, 6, 4, 7).reshape(rows, GROUP * part).astype(f32)
            for at in range(2)
        ]

    def kernel(ref, gate_ref, up_ref):
        for place, here, there in unit_chunks(unit):
            gate_ref[:, there : there + unit] = ref[place, :, here : here + unit].astype(f32)
            up_ref[:, there : there + unit] = ref[place, :, here + TILE : here + TILE + unit].astype(f32)

    whole = jax.ShapeDtypeStruct((rows, GROUP * part), f32)
    return pl.pallas_call(kernel, out_shape=[whole, whole], name="unpack_units")(shares)


def triangle(length):
    rows = lax.broadcasted_iota(jnp.int32, (length, length), 0)
    cols = lax.broadcasted_iota(jnp.int32, (length, length), 1)
    return rows >= cols


def decays(forget_pre, tri):
    log_gate = jax.nn.log_sigmoid(forget_pre)
    highest = lax.Precision.HIGHEST
    down = jnp.dot(tri, log_gate, preferred_element_type=f32, precision=highest)
    across = lax.dot_general(
        log_gate, tri, (((0,), (1,)), ((), ())), preferred_element_type=f32, precision=highest
    )
    return down, across


def half_mask(half):
    lane = lax.broadcasted_iota(jnp.int32, (1, LANES), 1)
    return (lane >= HEAD) == bool(half)


def attend_kernel(q_ref, k_ref, v_ref, gate_ref, forget_ref, seg_col, seg_row, gated_ref, attended_ref, log_ref):
    length = q_ref.shape[0]
    causal = triangle(length)
    down, across = decays(forget_ref[...], causal.astype(f32))
    bias = jnp.where(causal & (seg_col[...] == seg_row[0]), 0.0, negative_big)
    lane = lax.broadcasted_iota(jnp.int32, (length, LANES), 1)
    logs = jnp.zeros((length, LANES), f32)
    for pair in range(LOCAL_HEADS // 2):
        cols = slice(pair * LANES, (pair + 1) * LANES)
        query, key, value = q_ref[:, cols], k_ref[:, cols], v_ref[:, cols].astype(bf16)
        both = []
        for half in range(2):
            head = 2 * pair + half
            mine = half_mask(half)
            scaled = jnp.where(mine, query, 0) * jnp.asarray(0.125, bf16)
            scores = product_nt(scaled, key) + down[:, head : head + 1] - across[head : head + 1, :] + bias
            top = jnp.max(scores, -1, keepdims=True)
            shifted = jnp.exp(scores - top)
            total = jnp.sum(shifted, -1, keepdims=True)
            probs = (shifted * (1.0 / total)).astype(bf16)
            both.append(jnp.where(mine, product(probs, value), 0.0))
            logs = jnp.where(lane == head, top + jnp.log(total), logs)
        attended = both[0] + both[1]
        attended_ref[:, cols] = attended
        gated_ref[:, cols] = (attended * jax.nn.sigmoid(gate_ref[:, cols])).astype(bf16)
    log_ref[...] = logs


def attend_back_kernel(
    q_ref, k_ref, v_ref, gate_ref, forget_ref, seg_col, seg_row, attended_ref, log_ref, grad_ref,
    dq_ref, dk_ref, dv_ref, dgate_ref, dforget_ref,
):
    length = q_ref.shape[0]
    causal = triangle(length)
    tri = causal.astype(f32)
    down, across = decays(forget_ref[...], tri)
    bias = jnp.where(causal & (seg_col[...] == seg_row[0]), 0.0, negative_big)
    lane = lax.broadcasted_iota(jnp.int32, (length, LANES), 1)
    grad_decay = jnp.zeros((length, LANES), f32)
    for pair in range(LOCAL_HEADS // 2):
        cols = slice(pair * LANES, (pair + 1) * LANES)
        query, key, value = q_ref[:, cols], k_ref[:, cols], v_ref[:, cols].astype(bf16)
        out_gate = jax.nn.sigmoid(gate_ref[:, cols])
        grad_gated = grad_ref[:, cols]
        grad_att = (grad_gated * out_gate).astype(bf16)
        dgate_ref[:, cols] = (
            grad_gated * attended_ref[:, cols] * out_gate * (1.0 - out_gate)
        ).astype(bf16)
        dq, dk, dv = [], [], []
        for half in range(2):
            head = 2 * pair + half
            mine = half_mask(half)
            scaled = jnp.where(mine, query, 0) * jnp.asarray(0.125, bf16)
            scores = product_nt(scaled, key) + down[:, head : head + 1] - across[head : head + 1, :] + bias
            probs = jnp.exp(scores - log_ref[:, head : head + 1])
            grad_prob = product_nt(jnp.where(mine, grad_att, 0), value)
            delta = jnp.sum(probs * grad_prob, -1, keepdims=True)
            grad_scores = (probs * (grad_prob - delta)).astype(bf16)
            dq.append(product(grad_scores, key))
            dk.append(product_tn(grad_scores, query))
            dv.append(product_tn(probs.astype(bf16), grad_att))
            one = (lane == head).astype(bf16)
            grad_decay = grad_decay + product(grad_scores, one) - product_tn(grad_scores, one)
        first = half_mask(0)
        dq_ref[:, cols] = (jnp.where(first, dq[0], dq[1]) * 0.125).astype(bf16)
        dk_ref[:, cols] = (jnp.where(first, dk[0], dk[1]) * 0.125).astype(bf16)
        dv_ref[:, cols] = jnp.where(first, dv[0], dv[1]).astype(bf16)
    later = product_tn(tri, grad_decay, lax.Precision.HIGHEST)
    dforget_ref[...] = (later * jax.nn.sigmoid(-forget_ref[...])).astype(bf16)


def attention_specs(length, width):
    def columns(at):
        return pl.BlockSpec((length, width), lambda i: (i, at))

    lanes = pl.BlockSpec((length, LANES), lambda i: (i, 0))
    seg_col = pl.BlockSpec((length, 1), lambda i: (i, 0))
    seg_row = pl.BlockSpec((1, 1, length), lambda i: (i, 0, 0))
    return columns, lanes, seg_col, seg_row


def attend(query_key, value_gate, forget_pre, seg_col, seg_row, length):
    tokens, width = query_key.shape[0], query_key.shape[1] // 2
    columns, lanes, col_spec, row_spec = attention_specs(length, width)
    return pl.pallas_call(
        attend_kernel,
        grid=(tokens // length,),
        in_specs=[columns(0), columns(1), columns(0), columns(1), lanes, col_spec, row_spec],
        out_specs=[columns(0), columns(0), lanes],
        out_shape=[
            jax.ShapeDtypeStruct((tokens, width), bf16),
            jax.ShapeDtypeStruct((tokens, width), f32),
            jax.ShapeDtypeStruct((tokens, LANES), f32),
        ],
        compiler_params=kernel_params,
        cost_estimate=pl.CostEstimate(
            flops=4 * tokens * length * width, bytes_accessed=14 * tokens * width, transcendentals=0
        ),
        name="attend",
    )(query_key, query_key, value_gate, value_gate, forget_pre, seg_col, seg_row)


def attend_back(query_key, value_gate, forget_pre, seg_col, seg_row, attended, logs, grad_gated, length):
    tokens, width = query_key.shape[0], query_key.shape[1] // 2
    columns, lanes, col_spec, row_spec = attention_specs(length, width)
    whole = jax.ShapeDtypeStruct((tokens, width), bf16)
    return pl.pallas_call(
        attend_back_kernel,
        grid=(tokens // length,),
        in_specs=[
            columns(0), columns(1), columns(0), columns(1), lanes, col_spec, row_spec,
            columns(0), lanes, columns(0),
        ],
        out_specs=[columns(0), columns(0), columns(0), columns(0), lanes],
        out_shape=[whole, whole, whole, whole, jax.ShapeDtypeStruct((tokens, LANES), bf16)],
        compiler_params=kernel_params,
        cost_estimate=pl.CostEstimate(
            flops=10 * tokens * length * width, bytes_accessed=28 * tokens * width, transcendentals=0
        ),
        name="attend_back",
    )(query_key, query_key, value_gate, value_gate, forget_pre, seg_col, seg_row, attended, logs, grad_gated)


def ffn_kernel(hidden_ref, out_grad_ref, both_ref, down_ref, act_ref, dboth_ref, dhidden_ref, total):
    step = pl.program_id(0)
    both_weight, down_weight = both_ref[...], down_ref[...]
    both = product(hidden_ref[...], both_weight)
    gate_ffn, up_ffn = both[:, :TILE], both[:, TILE:]
    grad_act = product_nt(out_grad_ref[...], down_weight)
    sigmoid_gate = jax.nn.sigmoid(gate_ffn)
    silu = gate_ffn * sigmoid_gate
    act_ref[...] = (silu * up_ffn).astype(bf16)
    grad_gate = grad_act * up_ffn * sigmoid_gate * (1.0 + gate_ffn * (1.0 - sigmoid_gate))
    dboth_ref[:, :TILE] = grad_gate.astype(bf16)
    dboth_ref[:, TILE:] = (grad_act * silu).astype(bf16)
    term = product_nt(dboth_ref[...], both_weight)

    @pl.when(step == 0)
    def _():
        total[...] = term

    @pl.when(step > 0)
    def _():
        total[...] += term

    @pl.when(step == pl.num_programs(0) - 1)
    def _():
        dhidden_ref[...] = total[...].astype(bf16)


def feed_forward(hidden, out_grad, weight_both, weight_down):
    tokens, width = hidden.shape
    units = weight_down.shape[0]
    whole = pl.BlockSpec((tokens, width), lambda j: (0, 0))
    return pl.pallas_call(
        ffn_kernel,
        grid=(units // TILE,),
        in_specs=[
            whole,
            whole,
            pl.BlockSpec((width, 2 * TILE), lambda j: (0, j)),
            pl.BlockSpec((TILE, width), lambda j: (j, 0)),
        ],
        out_specs=[
            pl.BlockSpec((tokens, TILE), lambda j: (0, j)),
            pl.BlockSpec((tokens, 2 * TILE), lambda j: (0, j)),
            whole,
        ],
        out_shape=[
            jax.ShapeDtypeStruct((tokens, units), bf16),
            jax.ShapeDtypeStruct((tokens, 2 * units), bf16),
            jax.ShapeDtypeStruct((tokens, width), bf16),
        ],
        scratch_shapes=[pltpu.VMEM((tokens, width), f32)],
        compiler_params=kernel_params,
        cost_estimate=pl.CostEstimate(
            flops=10 * tokens * width * units, bytes_accessed=16 * tokens * width, transcendentals=0
        ),
        name="feed_forward",
    )(hidden, out_grad, weight_both, weight_down)


def shards(
    inputs,
    segment_ids,
    norm_one,
    w_query,
    w_key,
    w_value,
    w_gate_out,
    w_forget,
    forget_bias,
    w_output,
    norm_two,
    w_ffn_gate,
    w_ffn_up,
    w_ffn_down,
    out_grad,
):
    length, width = inputs.shape
    rows, unit = norm_one.shape[0], w_ffn_down.shape[0]
    size_w, size_r = lax.axis_size("w"), lax.axis_size("r")
    devices = math.prod(lax.axis_size(axis) for axis in ALL)
    place = lax.axis_index("c") * 2 + lax.axis_index("x")
    part = width // GROUP
    units = w_ffn_gate.shape[1] // GROUP

    heads_block = exchange(pack_heads((w_query, w_key, w_value, w_gate_out)), ("c", "x"))
    output_block = transpose_quarters(w_output)
    units_block = exchange(pack_units(w_ffn_gate, w_ffn_up, unit), ("y", "c"))
    seg_all = group_gather(segment_ids.astype(f32), "x")
    seg_col, seg_row = seg_all.reshape(-1, 1), seg_all[:, None, :]

    small = jnp.concatenate(
        (w_forget, norm_one[:, None], norm_two[:, None], jnp.zeros((rows, LANES - H - 2), bf16)), 1
    )
    small = exchange(jnp.broadcast_to(small[None], (devices, rows, LANES)), ALL).reshape(width, LANES)
    gain_one, gain_two = small[:, H].astype(f32), small[:, H + 1].astype(f32)
    forget_weight = lax.dynamic_slice(small, (0, place * LOCAL_HEADS), (width, LOCAL_HEADS))
    forget_weight = jnp.pad(forget_weight, ((0, 0), (0, LANES - LOCAL_HEADS)))
    bias_part = lax.dynamic_slice(forget_bias, (place * LOCAL_HEADS,), (LOCAL_HEADS,)).astype(f32)
    bias_part = jnp.pad(bias_part, (0, LANES - LOCAL_HEADS))

    attn = [jnp.concatenate((over_rest(heads_block.reshape(4 * rows, width)), over_rest(output_block)), 2)]
    down = [over_rest(w_ffn_down)]
    both = [over_rest(units_block.reshape(4 * rows, 2 * units))]
    attn_y, down_x, both_x = [], [swap(down[0], "x")], []

    down.append(along_z(down[0]))
    attn.append(along_z(attn[0]))
    attn_y.append(swap(attn[0], "y"))
    inputs_x = swap(inputs, "x")

    attn[1], both[0] = order((attn[1], both[0]), (attn_y[0], down[1]))
    attn.append(along_z(attn[1]))
    attn_y.append(swap(attn[1], "y"))
    both_x.append(swap(both[0], "x"))

    attn[2], down[1] = order((attn[2], down[1]), (attn_y[1], inputs_x))
    attn.append(along_z(attn[2]))
    attn_y.append(swap(attn[2], "y"))
    down_x.append(swap(down[1], "x"))

    attn[3], both[0] = order((attn[3], both[0]), (attn_y[2], both_x[0]))
    attn_y.append(swap(attn[3], "y"))
    both.append(along_z(both[0]))
    down.append(along_z(down[1]))
    out_grad_y = swap(out_grad, "y")

    both[1], down[2] = order((both[1], down[2]), (attn_y[3], down_x[1]))
    both.append(along_z(both[1]))
    both_x.append(swap(both[1], "x"))

    def arrivals(own, across):
        return [(step, other, (own, across)[other][step]) for step in range(Z) for other in range(2)]

    def attn_order(whole):
        heads = whole[:, :, :, :, : 4 * rows].reshape(Z, 2, size_w, size_r, 2, 2, rows, width)
        out = whole[:, :, :, :, 4 * rows :].reshape(2, 2, 2, size_w, size_r, rows, width)
        return (
            heads.transpose(0, 2, 1, 4, 3, 5, 6, 7).reshape(width, width),
            out.transpose(3, 2, 0, 4, 1, 5, 6).reshape(part, width),
        )

    def attn_spots(outs, at_z, at_y):
        yield outs[0], 0, 4 * rows, outs[0].at[pl.ds(pl.multiple_of((at_z * 2 + at_y) * 4 * rows, rows), 4 * rows)]
        yield outs[1], 4 * rows, rows, outs[1].at[pl.ds(pl.multiple_of((at_y * 4 + at_z) * rows, rows), rows)]

    weight_heads, weight_out = arrange(
        arrivals(attn, attn_y), "y", ((width, width), (part, width)), attn_order, attn_spots
    )

    inputs_all = jnp.concatenate((inputs, inputs_x, swap(inputs, "c"), swap(inputs_x, "c")), 0)
    out_grad_all = jnp.concatenate((out_grad, out_grad_y, swap(out_grad, "c"), swap(out_grad_y, "c")), 0)
    hidden_one = (row_norm(inputs_all.astype(f32))[0] * gain_one).astype(bf16)
    query_key = product(hidden_one, weight_heads[:, : 2 * part]).astype(bf16)
    value_gate = product(hidden_one, weight_heads[:, 2 * part :])
    forget_pre = product(hidden_one, forget_weight) + bias_part

    both[2], down[2], query_key = order((both[2], down[2], query_key), (both_x[1],))
    both.append(along_z(both[2]))
    down.append(along_z(down[2]))
    both_x.append(swap(both[2], "x"))

    gated_att, attended, logs = attend(query_key, value_gate, forget_pre, seg_col, seg_row, length)
    tokens = inputs.astype(f32)
    middle = tokens + group_scatter(product(gated_att, weight_out).astype(bf16), "x")
    normed_two, inv_two = row_norm(middle)
    hidden_own = (normed_two * gain_two).astype(bf16)

    both[3], down[2], down[3] = order((both[3], down[2], down[3]), (hidden_own, both_x[2]))
    both_x.append(swap(both[3], "x"))
    down_x += [swap(down[2], "x"), swap(down[3], "x")]
    hidden_two = group_gather(hidden_own, "y")

    def down_order(whole):
        return (whole.reshape(units, width),)

    def down_spots(outs, at_z, at_x):
        yield outs[0], 0, unit, outs[0].at[pl.ds(pl.multiple_of((at_z * 2 + at_x) * unit, unit), unit)]

    (weight_down,) = arrange(arrivals(down, down_x), "x", ((units, width),), down_order, down_spots)

    def both_order(whole):
        split = whole.reshape(Z, 2, size_w, size_r, 2, 2, rows, 2 * units)
        return (split.transpose(0, 2, 4, 5, 3, 1, 6, 7).reshape(width, 2 * units),)

    def both_spots(outs, at_z, at_x):
        for at in range(GROUP):
            first = pl.multiple_of(((at_z * GROUP + at) * 2 + at_x) * rows, rows)
            yield outs[0], at * rows, rows, outs[0].at[pl.ds(first, rows)]

    (weight_both,) = arrange(arrivals(both, both_x), "x", ((width, 2 * units),), both_order, both_spots)

    activation, grad_both, grad_hidden = feed_forward(hidden_two, out_grad_all, weight_both, weight_down)

    def down_part(term):
        split = term.reshape(Z, 2, size_w, size_r, unit, width)
        return lambda at_z, at_x: lax.dynamic_slice(
            split, (at_z, at_x, 0, 0, 0, 0), (1, 1, *split.shape[2:])
        )[0, 0]

    def both_part(term):
        split = term.reshape(Z, size_w, 4, size_r, 2, rows, 2 * units)

        def piece(at_z, at_x):
            size = (1, size_w, 4, size_r, 1, rows, 2 * units)
            found = lax.dynamic_slice(split, (at_z, 0, 0, 0, at_x, 0, 0), size)[0, :, :, :, 0]
            return found.transpose(0, 2, 1, 3, 4).reshape(size_w, size_r, 4 * rows, 2 * units)

        return piece

    quarter = grad_hidden.shape[0] // GROUP
    near = grad_hidden[: 2 * quarter].astype(f32) + swap(grad_hidden[2 * quarter :], "c").astype(f32)
    near_own, near_sent = near[:quarter], near[quarter:].astype(bf16)
    down_halves = halves(down_part(product_tn(activation, out_grad_all).astype(bf16)), "x")
    down_got = [swap(down_halves[0][0], "x")]
    near_sent, grad_both = order((near_sent, grad_both), (down_halves[0][0],))
    grad_hidden_two = near_own + swap(near_sent, "y").astype(f32)
    both_halves = halves(both_part(product_tn(hidden_two, grad_both).astype(bf16)), "x")
    both_got = [swap(both_halves[0][0], "x")]
    layer_partial = product(activation, weight_down).astype(bf16)

    grad_middle = out_grad.astype(f32) + norm_back(grad_hidden_two * gain_two, normed_two, inv_two)
    grad_branch = grad_middle.astype(bf16)
    branch_x = swap(grad_branch, "x")
    down_total = down_halves[0][1]() + down_got[0].astype(f32)
    both_total = both_halves[0][1]() + both_got[0].astype(f32)
    down_sent, both_sent, layer_partial = order(
        (down_total.astype(bf16), both_total.astype(bf16), layer_partial), (grad_branch,)
    )
    down_z, both_z = along_z(down_sent), along_z(both_sent)
    layer_output = (middle + group_scatter(layer_partial, "y")).astype(bf16)

    sent = order((down_halves[1][0], both_halves[1][0]), (branch_x,))
    down_got.append(swap(sent[0], "x"))
    both_got.append(swap(sent[1], "x"))
    grad_branch = jnp.concatenate((grad_branch, branch_x, swap(grad_branch, "c"), swap(branch_x, "c")), 0)

    grad_gated = product_nt(grad_branch, weight_out)
    grad_gated, down_z, both_z = order((grad_gated, down_z, both_z), ())
    grad_query, grad_key, grad_value, grad_gate_pre, grad_forget = attend_back(
        query_key, value_gate, forget_pre, seg_col, seg_row, attended, logs, grad_gated, length
    )

    down_total = down_halves[1][1]() + down_got[1].astype(f32) + down_z.astype(f32)
    both_total = both_halves[1][1]() + both_got[1].astype(f32) + both_z.astype(f32)
    sent = order(
        (down_total.astype(bf16), both_total.astype(bf16), down_halves[2][0], both_halves[2][0]), (grad_query,)
    )
    down_z, both_z = along_z(sent[0]), along_z(sent[1])
    down_got.append(swap(sent[2], "x"))
    both_got.append(swap(sent[3], "x"))

    grad_heads = jnp.concatenate((grad_query, grad_key, grad_value, grad_gate_pre), 1)
    heads_term = product_tn(hidden_one, grad_heads).astype(bf16)
    out_term = product_tn(gated_att, grad_branch).astype(bf16)

    def attn_part(at_z, at_y):
        heads = heads_term.reshape(Z, size_w, 2, 2, size_r, 2, rows, width)
        heads = lax.dynamic_slice(heads, (at_z, 0, at_y, 0, 0, 0, 0, 0), (1, size_w, 1, 2, size_r, 2, rows, width))
        heads = heads[0, :, 0].transpose(0, 2, 1, 3, 4, 5).reshape(size_w, size_r, 4 * rows, width)
        out = out_term.reshape(size_w, 2, 2, size_r, 2, rows, width)
        out = lax.dynamic_slice(out, (0, at_y, at_z // 2, 0, at_z % 2, 0, 0), (size_w, 1, 1, size_r, 1, rows, width))
        return jnp.concatenate((heads, out.reshape(size_w, size_r, rows, width)), 2)

    attn_halves = halves(attn_part, "y")
    attn_got = [swap(send, "y") for send, _ in attn_halves]
    hidden_partial = product_nt(grad_heads, weight_heads) + product_nt(grad_forget, forget_weight)
    grad_hidden_one = group_scatter(hidden_partial.astype(bf16), "x")

    for step in (2, 3):
        down_total = down_halves[step][1]() + down_got[step].astype(f32) + down_z.astype(f32)
        both_total = both_halves[step][1]() + both_got[step].astype(f32) + both_z.astype(f32)
        if step == 2:
            sent = (down_total.astype(bf16), both_total.astype(bf16), down_halves[3][0], both_halves[3][0])
            down_z, both_z = along_z(sent[0]), along_z(sent[1])
            down_got.append(swap(sent[2], "x"))
            both_got.append(swap(sent[3], "x"))
    ffn_down_grad = sum_over_rest(down_total)
    both_block = sum_over_rest(both_total).astype(bf16).reshape(4, rows, 2 * units)
    ffn_gate_grad, ffn_up_grad = unpack_units(exchange(both_block, ("y", "c")), unit)

    attn_total = attn_halves[0][1]() + attn_got[0].astype(f32)
    for step in range(1, Z):
        attn_z = along_z(attn_total.astype(bf16))
        attn_total = attn_halves[step][1]() + attn_got[step].astype(f32) + attn_z.astype(f32)
    attn_sum = sum_over_rest(attn_total).astype(bf16)
    w_output_grad = transpose_quarters(attn_sum[4 * rows :]).astype(f32)
    query_grad, key_grad, value_grad, gate_out_grad = unpack_heads(
        exchange(attn_sum[: 4 * rows].reshape(4, rows, width), ("c", "x")), 4
    )

    def scatter_vector(partial, extra=None):
        sent = partial.reshape(devices, rows)
        if extra is not None:
            sent = jnp.concatenate((sent, jnp.broadcast_to(extra[None], (devices, extra.shape[0]))), 1)
        return jnp.sum(exchange(sent, ALL), 0)

    norm_two_grad = scatter_vector(jnp.sum(grad_hidden_two * normed_two, 0))
    forget_term = product_tn(grad_forget, hidden_one)[:8]

    forget_got = exchange(forget_term.reshape(8, devices, rows).transpose(1, 0, 2), ALL)
    forget_got = forget_got.reshape(Z, size_w, 2, 2, size_r, 2, 8, rows).sum((0, 1, 2, 4))
    forget_grad = forget_got[:, :, :LOCAL_HEADS].reshape(H, rows).T

    bias_sum = jnp.sum(grad_forget.astype(f32), 0)[:LOCAL_HEADS]
    bias_sum = lax.dynamic_update_slice(jnp.zeros((H,), f32), bias_sum, (place * LOCAL_HEADS,))
    normed, inv_one = row_norm(tokens)
    last = scatter_vector(jnp.sum(grad_hidden_one * normed, 0), bias_sum)
    norm_one_grad, forget_bias_grad = last[:rows], last[rows:]
    input_grad = grad_middle + norm_back(grad_hidden_one * gain_one, normed, inv_one)
    return (
        layer_output,
        input_grad,
        norm_one_grad,
        query_grad,
        key_grad,
        value_grad,
        gate_out_grad,
        forget_grad,
        forget_bias_grad,
        w_output_grad,
        norm_two_grad,
        ffn_gate_grad,
        ffn_up_grad,
        ffn_down_grad,
    )


def solution(mesh):
    fsdp, rep = mesh.shape["fsdp"], mesh.shape["rep"]
    finer = Mesh(mesh.devices.reshape(Z, fsdp // 16, 2, 2, rep // 2, 2), ALL)
    rows, line = P(ALL, None), P(ALL)
    in_specs = (
        rows, rows, line, rows, rows, rows, rows, rows, P(), rows, line, rows, rows, rows, rows,
    )
    out_specs = (
        rows, rows, line, rows, rows, rows, rows, rows, P(), rows, line, rows, rows, rows,
    )
    return jax.shard_map(shards, mesh=finer, in_specs=in_specs, out_specs=out_specs, check_vma=False)
```

```python
import math

import jax
import jax.numpy as jnp
from jax import lax
from jax.experimental import pallas as pl
from jax.experimental.pallas import tpu as pltpu
from jax.sharding import Mesh
from jax.sharding import PartitionSpec as P

H = 24
HEAD = 64
Z = 4
GROUP = 4
LANES = 128
TILE = 256
LOCAL_HEADS = H // GROUP

epsilon = 1e-06
negative_big = -1e30
bf16 = jnp.bfloat16
f32 = jnp.float32
ALL = ("z", "w", "y", "c", "r", "x")
REST = ("w", "r")
ANY = pl.BlockSpec(memory_space=pl.ANY)
kernel_params = pltpu.CompilerParams(vmem_limit_bytes=48 * 1024 * 1024)


def row_norm(tokens):
    inverse_rms = lax.rsqrt(jnp.mean(tokens * tokens, -1, keepdims=True) + epsilon)
    return (tokens * inverse_rms, inverse_rms)


def norm_back(grad_hat, normed, inverse_rms):
    return inverse_rms * (grad_hat - normed * jnp.mean(grad_hat * normed, -1, keepdims=True))


def product(left, right):
    return jnp.dot(left, right, preferred_element_type=f32)


def product_nt(left, right, precision=None):
    return lax.dot_general(
        left, right, (((1,), (1,)), ((), ())), preferred_element_type=f32, precision=precision
    )


def product_tn(left, right, precision=None):
    return lax.dot_general(
        left, right, (((0,), (0,)), ((), ())), preferred_element_type=f32, precision=precision
    )


def place_in_ring(index):
    return index ^ (index >> 1)


def found_at(step):
    return place_in_ring((place_in_ring(lax.axis_index("z")) - step) & 3)


def along_z(block):
    return lax.ppermute(block, "z", [(0, 1), (1, 3), (3, 2), (2, 0)])


def swap(value, axis):
    return lax.ppermute(value, axis, [(0, 1), (1, 0)])


def has_rest():
    return lax.axis_size("w") * lax.axis_size("r") > 1


def over_rest(block):
    if not has_rest():
        return block[None, None]
    return lax.all_gather(lax.all_gather(block, "r"), "w")


def sum_over_rest(total):
    if not has_rest():
        return total[0, 0]
    return lax.psum_scatter(lax.psum_scatter(total, "w"), "r")


def order(values, after):
    count = len(values)
    if has_rest():
        return values
    return pl.pallas_call(
        lambda *refs: None,
        in_specs=[ANY] * (count + len(after)),
        out_specs=[ANY] * count,
        out_shape=[jax.ShapeDtypeStruct(value.shape, value.dtype) for value in values],
        input_output_aliases={at: at for at in range(count)},
        name="order",
    )(*values, *after)


def arrange(arrivals, axis, shape, reorder, spots):
    mine = lax.axis_index(axis)
    blocks = [block for _, _, block in arrivals]
    if has_rest():
        whole = jnp.zeros((Z, 2, *blocks[0].shape), blocks[0].dtype)
        for step, other, block in arrivals:
            at = (found_at(step), mine ^ other)
            whole = lax.dynamic_update_slice(whole, block[None, None], (*at, *[0] * block.ndim))
        return reorder(whole)
    blocks = [block.reshape(-1, block.shape[-1]) for block in blocks]
    places = jnp.stack([found_at(step) for step in range(Z)] + [mine, 1 - mine]).astype(jnp.int32)

    def kernel(places_ref, *refs):
        block_refs, outs, sems = refs[: len(blocks)], refs[len(blocks) : -1], refs[-1]
        copies = []
        for at, (step, other, _) in enumerate(arrivals):
            for out, first, rows, spot in spots(outs, places_ref[step], places_ref[Z + other]):
                source = block_refs[at].at[pl.ds(first, rows)]
                copies.append(pltpu.make_async_copy(source, spot, sems.at[len(copies)]))
        for copy in copies:
            copy.start()
        for copy in copies:
            copy.wait()

    return pl.pallas_call(
        kernel,
        in_specs=[pl.BlockSpec(memory_space=pltpu.SMEM)]
        + [pl.BlockSpec(memory_space=pltpu.VMEM)] * len(blocks),
        out_specs=[ANY] * len(shape),
        out_shape=[jax.ShapeDtypeStruct(one, bf16) for one in shape],
        scratch_shapes=[pltpu.SemaphoreType.DMA((8 * len(blocks),))],
        compiler_params=kernel_params,
        name="arrange",
    )(places, *blocks)


def group_gather(own, axis):
    over = swap(own, axis)
    return jnp.concatenate((own, swap(own, "c"), over, swap(over, "c")), 0)


def near_sum(partial):
    rows = partial.shape[0] // 2
    return partial[:rows].astype(f32) + swap(partial[rows:], "c").astype(f32)


def group_scatter(partial, axis):
    rows = partial.shape[0] // 2
    over = swap(near_sum(partial[rows:]).astype(bf16), axis)
    return near_sum(partial[:rows]) + over.astype(f32)


def exchange(shares, axes):
    return lax.all_to_all(shares, axes, 0, 0, tiled=True)


def transpose_quarters(block):
    return lax.ppermute(
        block, ("z", "c", "x"), [(i * GROUP + j, j * GROUP + i) for i in range(Z) for j in range(GROUP)]
    )


def gather_units(block):
    if has_rest():
        block = lax.all_gather(block, "r", axis=1)
    return lax.all_gather(block.reshape(-1, block.shape[-1]), ("z", "w", "y"), axis=0, tiled=True)


def units_halves(grad):
    if has_rest():
        return grad, None
    parts = grad.reshape(Z, 2, -1, grad.shape[1])
    mine = lax.axis_index("y")
    sent = lax.dynamic_slice_in_dim(parts, 1 - mine, 1, 1).reshape(-1, grad.shape[1])
    return lax.dynamic_slice_in_dim(parts, mine, 1, 1).reshape(-1, grad.shape[1]), sent


def scatter_units(total, halves, rows, axes):
    if not has_rest():
        return lax.psum_scatter(total, axes, scatter_dimension=0, tiled=True)
    kept = lax.psum_scatter(total, ("z", "w", "y"), scatter_dimension=0, tiled=True)
    kept = kept.reshape(halves, -1, halves, rows, kept.shape[-1])
    return lax.psum_scatter(kept, "r", scatter_dimension=1).reshape(-1, kept.shape[-1])


def pack_heads(weights):
    rows, width = weights[0].shape
    part = width // GROUP

    def kernel(*refs):
        for at, ref in enumerate(refs[:-1]):
            for to in range(GROUP):
                refs[-1][to, :, at * part : (at + 1) * part] = ref[:, to * part : (to + 1) * part]

    return pl.pallas_call(
        kernel, out_shape=jax.ShapeDtypeStruct((GROUP, rows, len(weights) * part), bf16), name="pack_heads"
    )(*weights)


def unpack_heads(shares, count):
    rows, part = shares.shape[1], shares.shape[2] // count

    def kernel(ref, *outs):
        for at, out in enumerate(outs):
            for to in range(GROUP):
                out[:, to * part : (to + 1) * part] = ref[to, :, at * part : (at + 1) * part].astype(f32)

    whole = jax.ShapeDtypeStruct((rows, GROUP * part), f32)
    return pl.pallas_call(kernel, out_shape=[whole] * count, name="unpack_heads")(shares)


def unit_chunks(unit):
    for at in range(2 * Z):
        for place in range(GROUP):
            here = at * unit
            yield place, here // TILE * 2 * TILE + here % TILE, (at * GROUP + place) * unit


def pack_units(gate, up, unit):
    rows, hidden = gate.shape
    part = hidden // GROUP
    if has_rest():
        size = (rows, Z, lax.axis_size("w"), 2, 2, lax.axis_size("r"), 2, unit)
        both = [
            one.reshape(size).transpose(4, 6, 0, 1, 2, 3, 5, 7).reshape(GROUP, rows, part // TILE, TILE)
            for one in (gate, up)
        ]
        return jnp.stack(both, 3).reshape(GROUP, rows, 2 * part)

    def kernel(gate_ref, up_ref, out):
        for place, here, there in unit_chunks(unit):
            out[place, :, here : here + unit] = gate_ref[:, there : there + unit]
            out[place, :, here + TILE : here + TILE + unit] = up_ref[:, there : there + unit]

    return pl.pallas_call(
        kernel, out_shape=jax.ShapeDtypeStruct((GROUP, rows, 2 * part), bf16), name="pack_units"
    )(gate, up)


def unpack_units(shares, unit):
    rows, part = shares.shape[1], shares.shape[2] // 2
    if has_rest():
        size = (2, 2, rows, Z, lax.axis_size("w"), 2, lax.axis_size("r"), unit)
        both = shares.reshape(GROUP, rows, part // TILE, 2, TILE)
        return [
            both[:, :, :, at].reshape(size).transpose(2, 3, 4, 5, 0, 6, 1, 7).reshape(rows, GROUP * part).astype(f32)
            for at in range(2)
        ]

    def kernel(ref, gate_ref, up_ref):
        for place, here, there in unit_chunks(unit):
            gate_ref[:, there : there + unit] = ref[place, :, here : here + unit].astype(f32)
            up_ref[:, there : there + unit] = ref[place, :, here + TILE : here + TILE + unit].astype(f32)

    whole = jax.ShapeDtypeStruct((rows, GROUP * part), f32)
    return pl.pallas_call(kernel, out_shape=[whole, whole], name="unpack_units")(shares)


def triangle(length):
    rows = lax.broadcasted_iota(jnp.int32, (length, length), 0)
    cols = lax.broadcasted_iota(jnp.int32, (length, length), 1)
    return rows >= cols


def decays(forget_pre, tri):
    log_gate = jax.nn.log_sigmoid(forget_pre)
    highest = lax.Precision.HIGHEST
    down = jnp.dot(tri, log_gate, preferred_element_type=f32, precision=highest)
    across = lax.dot_general(
        log_gate, tri, (((0,), (1,)), ((), ())), preferred_element_type=f32, precision=highest
    )
    return down, across


def half_mask(half):
    lane = lax.broadcasted_iota(jnp.int32, (1, LANES), 1)
    return (lane >= HEAD) == bool(half)


def attend_kernel(q_ref, k_ref, v_ref, gate_ref, forget_ref, seg_col, seg_row, gated_ref, attended_ref, log_ref):
    length = q_ref.shape[0]
    causal = triangle(length)
    down, across = decays(forget_ref[...], causal.astype(f32))
    bias = jnp.where(causal & (seg_col[...] == seg_row[0]), 0.0, negative_big)
    lane = lax.broadcasted_iota(jnp.int32, (length, LANES), 1)
    logs = jnp.zeros((length, LANES), f32)
    for pair in range(LOCAL_HEADS // 2):
        cols = slice(pair * LANES, (pair + 1) * LANES)
        query, key, value = q_ref[:, cols], k_ref[:, cols], v_ref[:, cols].astype(bf16)
        both = []
        for half in range(2):
            head = 2 * pair + half
            mine = half_mask(half)
            scaled = jnp.where(mine, query, 0) * jnp.asarray(0.125, bf16)
            scores = product_nt(scaled, key) + down[:, head : head + 1] - across[head : head + 1, :] + bias
            top = jnp.max(scores, -1, keepdims=True)
            shifted = jnp.exp(scores - top)
            total = jnp.sum(shifted, -1, keepdims=True)
            probs = (shifted * (1.0 / total)).astype(bf16)
            both.append(jnp.where(mine, product(probs, value), 0.0))
            logs = jnp.where(lane == head, top + jnp.log(total), logs)
        attended = both[0] + both[1]
        attended_ref[:, cols] = attended
        gated_ref[:, cols] = (attended * jax.nn.sigmoid(gate_ref[:, cols])).astype(bf16)
    log_ref[...] = logs


def attend_back_kernel(
    q_ref, k_ref, v_ref, gate_ref, forget_ref, seg_col, seg_row, attended_ref, log_ref, grad_ref, heads_ref, dforget_ref,
):
    length, width = q_ref.shape
    causal = triangle(length)
    tri = causal.astype(f32)
    down, across = decays(forget_ref[...], tri)
    bias = jnp.where(causal & (seg_col[...] == seg_row[0]), 0.0, negative_big)
    lane = lax.broadcasted_iota(jnp.int32, (length, LANES), 1)
    grad_decay = jnp.zeros((length, LANES), f32)
    for pair in range(LOCAL_HEADS // 2):
        cols = slice(pair * LANES, (pair + 1) * LANES)
        query, key, value = q_ref[:, cols], k_ref[:, cols], v_ref[:, cols].astype(bf16)
        out_gate = jax.nn.sigmoid(gate_ref[:, cols])
        grad_gated = grad_ref[:, cols]
        grad_att = (grad_gated * out_gate).astype(bf16)
        grad_gate = (grad_gated * attended_ref[:, cols] * out_gate * (1.0 - out_gate)).astype(bf16)
        dq, dk, dv = [], [], []
        for half in range(2):
            head = 2 * pair + half
            mine = half_mask(half)
            scaled = jnp.where(mine, query, 0) * jnp.asarray(0.125, bf16)
            scores = product_nt(scaled, key) + down[:, head : head + 1] - across[head : head + 1, :] + bias
            probs = jnp.exp(scores - log_ref[:, head : head + 1])
            grad_prob = product_nt(jnp.where(mine, grad_att, 0), value)
            delta = jnp.sum(probs * grad_prob, -1, keepdims=True)
            grad_scores = (probs * (grad_prob - delta)).astype(bf16)
            dq.append(product(grad_scores, key))
            dk.append(product_tn(grad_scores, query))
            dv.append(product_tn(probs.astype(bf16), grad_att))
            one = (lane == head).astype(bf16)
            grad_decay = grad_decay + product(grad_scores, one) - product_tn(grad_scores, one)
        first = half_mask(0)
        found = (
            (jnp.where(first, dq[0], dq[1]) * 0.125).astype(bf16),
            (jnp.where(first, dk[0], dk[1]) * 0.125).astype(bf16),
            jnp.where(first, dv[0], dv[1]).astype(bf16),
            grad_gate,
        )
        for at, one in enumerate(found):
            heads_ref[:, at * width + pair * LANES : at * width + (pair + 1) * LANES] = one
    later = product_tn(tri, grad_decay, lax.Precision.HIGHEST)
    dforget_ref[...] = (later * jax.nn.sigmoid(-forget_ref[...])).astype(bf16)


def attention_specs(length, width, first):
    def columns(at):
        return pl.BlockSpec((length, width), lambda i: (first + i, at))

    lanes = pl.BlockSpec((length, LANES), lambda i: (first + i, 0))
    seg_col = pl.BlockSpec((length, 1), lambda i: (first + i, 0))
    seg_row = pl.BlockSpec((1, 1, length), lambda i: (first + i, 0, 0))
    return columns, lanes, seg_col, seg_row


def attend(query_key, value_gate, forget_pre, seg_col, seg_row, length):
    tokens, width = query_key.shape[0], query_key.shape[1] // 2
    columns, lanes, col_spec, row_spec = attention_specs(length, width, 0)
    return pl.pallas_call(
        attend_kernel,
        grid=(tokens // length,),
        in_specs=[columns(0), columns(1), columns(0), columns(1), lanes, col_spec, row_spec],
        out_specs=[columns(0), columns(0), lanes],
        out_shape=[
            jax.ShapeDtypeStruct((tokens, width), bf16),
            jax.ShapeDtypeStruct((tokens, width), f32),
            jax.ShapeDtypeStruct((tokens, LANES), f32),
        ],
        compiler_params=kernel_params,
        cost_estimate=pl.CostEstimate(
            flops=4 * tokens * length * width, bytes_accessed=14 * tokens * width, transcendentals=0
        ),
        name="attend",
    )(query_key, query_key, value_gate, value_gate, forget_pre, seg_col, seg_row)


def attend_back(query_key, value_gate, forget_pre, seg_col, seg_row, attended, logs, grad_gated, length, first):
    tokens, width = grad_gated.shape
    columns, lanes, col_spec, row_spec = attention_specs(length, width, first)
    own_columns, own_lanes, _, _ = attention_specs(length, width, 0)
    return pl.pallas_call(
        attend_back_kernel,
        grid=(tokens // length,),
        in_specs=[
            columns(0), columns(1), columns(0), columns(1), lanes, col_spec, row_spec,
            columns(0), lanes, own_columns(0),
        ],
        out_specs=[pl.BlockSpec((length, 4 * width), lambda i: (i, 0)), own_lanes],
        out_shape=[
            jax.ShapeDtypeStruct((tokens, 4 * width), bf16),
            jax.ShapeDtypeStruct((tokens, LANES), bf16),
        ],
        compiler_params=kernel_params,
        cost_estimate=pl.CostEstimate(
            flops=0, bytes_accessed=0, transcendentals=0
        ),
        name="attend_back",
    )(query_key, query_key, value_gate, value_gate, forget_pre, seg_col, seg_row, attended, logs, grad_gated)


def attn_terms(hidden, grad_heads, gated, grad_branch, rows):
    tokens, width = hidden.shape
    part, half = gated.shape[1], tokens // 2

    def both(left_ref, right_refs):
        near = product_tn(left_ref[:half, :], right_refs[0][...])
        return (near + product_tn(left_ref[half:, :], right_refs[1][...])).astype(bf16)

    def kernel(hidden_ref, near_ref, far_ref, gated_ref, branch_near, branch_far, out_ref, out_term):
        at_z = pl.program_id(0)

        @pl.when(at_z == 0)
        def _():
            out_term[...] = both(gated_ref, (branch_near, branch_far))

        term = both(hidden_ref, (near_ref, far_ref))
        for at_y in range(2):
            out_ref[at_y, : 4 * rows] = term[at_y * 4 * rows : (at_y + 1) * 4 * rows]
            first = pl.multiple_of((at_y * 4 + at_z) * rows, rows)
            out_ref[at_y, 4 * rows :] = out_term[pl.ds(first, rows), :]

    piece = pl.BlockSpec((half, width), lambda z: (0, 0))
    return pl.pallas_call(
        kernel,
        grid=(Z,),
        in_specs=[
            pl.BlockSpec((tokens, 8 * rows), lambda z: (0, z)),
            piece,
            piece,
            pl.BlockSpec((tokens, part), lambda z: (0, 0)),
            piece,
            piece,
        ],
        out_specs=pl.BlockSpec((2, 5 * rows, width), lambda z: (z, 0, 0)),
        out_shape=jax.ShapeDtypeStruct((2 * Z, 5 * rows, width), bf16),
        scratch_shapes=[pltpu.VMEM((part, width), bf16)],
        compiler_params=kernel_params,
        cost_estimate=pl.CostEstimate(
            flops=2 * tokens * width * (width + part), bytes_accessed=10 * tokens * width, transcendentals=0
        ),
        name="attn_terms",
    )(hidden, *grad_heads, gated, *grad_branch)


def back_through_heads(grad_heads, grad_forget, weight_heads, forget_weight):
    tokens, width = grad_heads.shape
    tile = width // 4

    def kernel(heads_ref, forget_ref, weight_ref, forget_weight_ref, out_ref):
        total = product_nt(heads_ref[...], weight_ref[...]) + product_nt(forget_ref[...], forget_weight_ref[...])
        out_ref[...] = total.astype(bf16)

    return pl.pallas_call(
        kernel,
        grid=(4,),
        in_specs=[
            pl.BlockSpec((tokens, width), lambda j: (0, 0)),
            pl.BlockSpec((tokens, LANES), lambda j: (0, 0)),
            pl.BlockSpec((tile, width), lambda j: (j, 0)),
            pl.BlockSpec((tile, LANES), lambda j: (j, 0)),
        ],
        out_specs=pl.BlockSpec((tokens, tile), lambda j: (0, j)),
        out_shape=jax.ShapeDtypeStruct((tokens, width), bf16),
        compiler_params=kernel_params,
        cost_estimate=pl.CostEstimate(
            flops=2 * tokens * width * width, bytes_accessed=8 * tokens * width, transcendentals=0
        ),
        name="back_through_heads",
    )(grad_heads, grad_forget, weight_heads, forget_weight)


def ffn_tile(hidden_ref, out_grad_ref, both_ref, down_ref, act_ref, dboth_ref):
    both = product(hidden_ref[...], both_ref[...])
    gate_ffn, up_ffn = both[:, :TILE], both[:, TILE:]
    grad_act = product_nt(out_grad_ref[...], down_ref[...])
    sigmoid_gate = jax.nn.sigmoid(gate_ffn)
    silu = gate_ffn * sigmoid_gate
    act_ref[...] = (silu * up_ffn).astype(bf16)
    grad_gate = grad_act * up_ffn * sigmoid_gate * (1.0 + gate_ffn * (1.0 - sigmoid_gate))
    dboth_ref[:, :TILE] = grad_gate.astype(bf16)
    dboth_ref[:, TILE:] = (grad_act * silu).astype(bf16)


def feed_forward(parts, out_grad, weight_both, weight_down):
    tokens, width = out_grad.shape
    units = weight_down.shape[0]
    steps = units // TILE
    whole = pl.BlockSpec((tokens, width), lambda j: (0, 0))
    rows = tokens // GROUP

    def kernel(*refs):
        joined = refs[GROUP + 3]

        @pl.when(pl.program_id(0) == 0)
        def _():
            for at in range(GROUP):
                joined[at * rows : (at + 1) * rows, :] = refs[at][...]

        ffn_tile(joined, *refs[GROUP : GROUP + 3], *refs[GROUP + 4 :])

    first = pl.BlockSpec((rows, width), lambda j: (0, 0))
    return pl.pallas_call(
        kernel,
        grid=(steps,),
        in_specs=[first] * GROUP
        + [
            whole,
            pl.BlockSpec((width, 2 * TILE), lambda j: (0, j)),
            pl.BlockSpec((TILE, width), lambda j: (j, 0)),
        ],
        out_specs=[
            whole,
            pl.BlockSpec((tokens, TILE), lambda j: (0, j)),
            pl.BlockSpec((tokens, 2 * TILE), lambda j: (0, j)),
        ],
        out_shape=[
            jax.ShapeDtypeStruct((tokens, width), bf16),
            jax.ShapeDtypeStruct((tokens, units), bf16),
            jax.ShapeDtypeStruct((tokens, 2 * units), bf16),
        ],
        compiler_params=kernel_params,
        cost_estimate=pl.CostEstimate(
            flops=6 * tokens * width * units, bytes_accessed=12 * tokens * width, transcendentals=0
        ),
        name="feed_forward",
    )(*parts, out_grad, weight_both, weight_down)


def shards(
    inputs,
    segment_ids,
    norm_one,
    w_query,
    w_key,
    w_value,
    w_gate_out,
    w_forget,
    forget_bias,
    w_output,
    norm_two,
    w_ffn_gate,
    w_ffn_up,
    w_ffn_down,
    out_grad,
):
    length, width = inputs.shape
    rows, unit = norm_one.shape[0], w_ffn_down.shape[0]
    size_w, size_r = lax.axis_size("w"), lax.axis_size("r")
    devices = math.prod(lax.axis_size(axis) for axis in ALL)
    place = lax.axis_index("c") * 2 + lax.axis_index("x")
    part = width // GROUP
    units = w_ffn_gate.shape[1] // GROUP
    far = 2 * length
    alone = not has_rest()

    heads_block = exchange(pack_heads((w_query, w_key, w_value, w_gate_out)), ("c", "x"))
    output_block = transpose_quarters(w_output)
    (units_shares,) = order((pack_units(w_ffn_gate, w_ffn_up, unit),), (heads_block,))
    units_block = exchange(units_shares, ("c", "x"))

    attn = [jnp.concatenate((over_rest(heads_block.reshape(4 * rows, width)), over_rest(output_block)), 2)]
    both = [units_block.reshape(4 * rows, 2 * units)]
    if alone:
        down_y = swap(w_ffn_down, "y")
        first = lax.axis_index("y") == 0
        down_pair = jnp.concatenate((jnp.where(first, w_ffn_down, down_y), jnp.where(first, down_y, w_ffn_down)), 0)
    else:
        down_pair = w_ffn_down
    (inputs_sent,) = order((inputs,), (heads_block, down_pair))
    inputs_x = swap(inputs_sent, "x")
    attn_y = [swap(attn[0], "y")]
    attn.append(along_z(attn[0]))

    (attn[1],) = order((attn[1],), (attn_y[0],))
    attn_y.append(swap(attn[1], "y"))
    attn.append(along_z(attn[1]))

    attn[2], out_grad_sent = order((attn[2], out_grad), (attn_y[1], inputs_x))
    out_grad_x = swap(out_grad_sent, "x")
    attn_y.append(swap(attn[2], "y"))
    attn.append(along_z(attn[2]))

    small = jnp.concatenate(
        (w_forget, norm_one[:, None], norm_two[:, None], jnp.zeros((rows, LANES - H - 2), bf16)), 1
    )
    (small,) = order((small,), (units_block,))
    seg_rows = length // LANES
    seg_own = jnp.pad(segment_ids.astype(bf16).reshape(seg_rows, LANES), ((0, 16 - seg_rows), (0, 0)))
    small = jnp.concatenate((small, seg_own), 0)
    small = exchange(jnp.broadcast_to(small[None], (devices, rows + 16, LANES)), ALL)
    small = small.reshape(devices, rows + 16, LANES)
    members = small[:, rows : rows + seg_rows].reshape(Z, size_w, 2, 2, size_r, 2, seg_rows, LANES)

    def member(other_x, other_c):
        at = [lax.axis_index(axis) for axis in ALL]
        at[5], at[3] = at[5] ^ other_x, at[3] ^ other_c
        return lax.dynamic_slice(members, (*at, 0, 0), (1, 1, 1, 1, 1, 1, seg_rows, LANES)).reshape(1, length)

    seg_all = jnp.concatenate((member(0, 0), member(0, 1), member(1, 0), member(1, 1)), 0).astype(f32)
    seg_col, seg_row = seg_all.reshape(-1, 1), seg_all[:, None, :]
    small = small[:, :rows].reshape(width, LANES)
    gain_one, gain_two = small[:, H].astype(f32), small[:, H + 1].astype(f32)
    forget_weight = lax.dynamic_slice(small, (0, place * LOCAL_HEADS), (width, LOCAL_HEADS))
    forget_weight = jnp.pad(forget_weight, ((0, 0), (0, LANES - LOCAL_HEADS)))
    bias_part = lax.dynamic_slice(forget_bias, (place * LOCAL_HEADS,), (LOCAL_HEADS,)).astype(f32)
    bias_part = jnp.pad(bias_part, (0, LANES - LOCAL_HEADS))

    attn[3], both[0], down_pair = order((attn[3], both[0], down_pair), (attn_y[2],))
    attn_y.append(swap(attn[3], "y"))
    both.append(along_z(both[0]))
    if alone:
        weight_down = lax.all_gather(down_pair, "z", axis=0, tiled=True)
    else:
        weight_down = gather_units(down_pair.reshape(1, 1, unit, width))

    def attn_order(whole):
        heads = whole[:, :, :, :, : 4 * rows].reshape(Z, 2, size_w, size_r, 2, 2, rows, width)
        out = whole[:, :, :, :, 4 * rows :].reshape(2, 2, 2, size_w, size_r, rows, width)
        return (
            heads.transpose(0, 2, 1, 4, 3, 5, 6, 7).reshape(width, width),
            out.transpose(3, 2, 0, 4, 1, 5, 6).reshape(part, width),
        )

    def attn_spots(outs, at_z, at_y):
        first = pl.multiple_of((at_z * 2 + at_y) * 4 * rows, 4 * rows)
        yield outs[0], 0, 4 * rows, outs[0].at[pl.ds(first, 4 * rows)]
        yield outs[1], 4 * rows, rows, outs[1].at[pl.ds(pl.multiple_of((at_y * 4 + at_z) * rows, rows), rows)]

    arrivals = [(step, other, (attn, attn_y)[other][step]) for step in range(Z) for other in range(2)]
    weight_heads, weight_out = arrange(arrivals, "y", ((width, width), (part, width)), attn_order, attn_spots)

    inputs_all = jnp.concatenate((inputs, swap(inputs, "c"), inputs_x, swap(inputs_x, "c")), 0)
    out_grad_all = jnp.concatenate((out_grad, swap(out_grad, "c"), out_grad_x, swap(out_grad_x, "c")), 0)
    hidden_one = (row_norm(inputs_all.astype(f32))[0] * gain_one).astype(bf16)

    hidden_one, both[0], both[1] = order((hidden_one, both[0], both[1]), (weight_out, out_grad_x))
    both_y = [None] * Z
    both_y[1] = swap(both[1], "y")
    both.append(along_z(both[1]))
    both_y[0] = swap(both[0], "y")
    query_key = product(hidden_one, weight_heads[:, : 2 * part]).astype(bf16)
    value_gate = product(hidden_one, weight_heads[:, 2 * part :])
    forget_pre = product(hidden_one, forget_weight) + bias_part
    gated_att, attended, logs = attend(query_key, value_gate, forget_pre, seg_col, seg_row, length)
    partial = product(gated_att, weight_out).astype(bf16)

    partial, both[2] = order((partial, both[2]), (both_y[1], out_grad_all))
    both_y[2] = swap(both[2], "y")
    both.append(along_z(both[2]))
    branch_x = swap(near_sum(partial[far:]).astype(bf16), "x")
    branch_near = near_sum(partial[:far])

    branch_x, branch_near, both[3] = order((branch_x, branch_near, both[3]), (both_y[0], both_y[2]))
    both_y[3] = swap(both[3], "y")
    tokens = inputs.astype(f32)
    middle = tokens + (branch_near + branch_x.astype(f32))
    normed_two, inv_two = row_norm(middle)
    hidden_own = (normed_two * gain_two).astype(bf16)
    hidden_x = swap(hidden_own, "x")
    hidden_parts = (hidden_own, swap(hidden_own, "c"), hidden_x, swap(hidden_x, "c"))
    if not alone:
        weight_both = gather_units(both[0].reshape(2, 2, rows, 2 * units))
    else:

        def both_spots(outs, at_z, at_y):
            first = pl.multiple_of((at_z * 2 + at_y) * 4 * rows, 4 * rows)
            yield outs[0], 0, 4 * rows, outs[0].at[pl.ds(first, 4 * rows)]

        arrivals = [(step, other, (both, both_y)[other][step]) for step in range(Z) for other in range(2)]
        (weight_both,) = arrange(arrivals, "y", ((width, 2 * units),), None, both_spots)

    hidden_two, activation, grad_both = feed_forward(hidden_parts, out_grad_all, weight_both, weight_down)
    both_term = product_tn(hidden_two, grad_both).astype(bf16)
    grad_both, activation = order((grad_both, activation), (both_term,))
    both_scattered = scatter_units(both_term, 2, rows, ("z", "y"))
    grad_hidden = product_nt(grad_both, weight_both).astype(bf16)
    near_sent = near_sum(grad_hidden[far:]).astype(bf16)
    grad_hidden_x = swap(near_sent, "x")
    near_own = near_sum(grad_hidden[:far])
    (activation,) = order((activation,), (near_sent,))
    kept_down, sent_down = units_halves(product_tn(activation, out_grad_all).astype(bf16))
    got_down = None if sent_down is None else swap(sent_down, "y")
    layer_partial = product(activation, weight_down).astype(bf16)
    grad_hidden_x, near_own = order(
        (grad_hidden_x, near_own), (layer_partial, kept_down if sent_down is None else sent_down)
    )

    grad_hidden_two = near_own + grad_hidden_x.astype(f32)
    grad_middle = out_grad.astype(f32) + norm_back(grad_hidden_two * gain_two, normed_two, inv_two)
    grad_own = grad_middle.astype(bf16)
    grad_c = swap(grad_own, "c")
    grad_x = swap(grad_own, "x")

    grad_near = jnp.concatenate((grad_own, grad_c), 0)

    def back(grad_branch, first):
        return attend_back(
            query_key, value_gate, forget_pre, seg_col, seg_row,
            attended, logs, product_nt(grad_branch, weight_out), length, first,
        )

    heads_near, forget_near = back(grad_near, 0)
    grad_x, heads_near, layer_partial = order((grad_x, heads_near, layer_partial), ())
    layer_output = (middle + group_scatter(layer_partial, "x")).astype(bf16)
    grad_far = jnp.concatenate((grad_x, swap(grad_x, "c")), 0)
    heads_far, forget_far = back(grad_far, 2)
    total_down = kept_down
    if got_down is not None:
        (got_down,) = order((got_down,), (heads_far,))
        total_down = (kept_down.astype(f32) + got_down.astype(f32)).astype(bf16)
    down_scattered = scatter_units(total_down, 1, unit, ("z",))

    if alone:
        terms = [attn_terms(hidden_one, (heads_near, heads_far), gated_att, (grad_near, grad_far), rows)]

        def attn_part(at_z, at_y):
            return lax.dynamic_index_in_dim(terms[-1], at_z * 2 + at_y, 0)[None]

    else:
        grad_heads = jnp.concatenate((heads_near, heads_far), 0)
        grad_branch = jnp.concatenate((grad_near, grad_far), 0)
        heads_term = product_tn(hidden_one, grad_heads).astype(bf16)
        out_term = product_tn(gated_att, grad_branch).astype(bf16)

        def attn_part(at_z, at_y):
            heads = heads_term.reshape(Z, size_w, 2, 2, size_r, 2, rows, width)
            size = (1, size_w, 1, 2, size_r, 2, rows, width)
            heads = lax.dynamic_slice(heads, (at_z, 0, at_y, 0, 0, 0, 0, 0), size)
            heads = heads[0, :, 0].transpose(0, 2, 1, 3, 4, 5).reshape(size_w, size_r, 4 * rows, width)
            out = out_term.reshape(size_w, 2, 2, size_r, 2, rows, width)
            size = (size_w, 1, 1, size_r, 1, rows, width)
            out = lax.dynamic_slice(out, (0, at_y, at_z // 2, 0, at_z % 2, 0, 0), size)
            return jnp.concatenate((heads, out.reshape(size_w, size_r, rows, width)), 2)

    other_y = 1 - lax.axis_index("y")
    attn_sent = attn_part(found_at(1), other_y)
    attn_got = [swap(attn_sent, "y")]
    heads_near, heads_far, forget_near, forget_far = order(
        (heads_near, heads_far, forget_near, forget_far), (attn_sent,)
    )
    if alone:
        terms += order((terms[0],), (attn_sent,))
    grad_forget = jnp.concatenate((forget_near, forget_far), 0)
    forget_term = product_tn(hidden_one, grad_forget).astype(bf16).reshape(devices, rows, LANES)
    forget_got = exchange(forget_term, ALL)
    bias_sum = jnp.sum(grad_forget.astype(f32), 0)[:LOCAL_HEADS]
    bias_sum = lax.dynamic_update_slice(jnp.zeros((H,), f32), bias_sum, (place * LOCAL_HEADS,))
    attn_later = [attn_part(found_at(step), other_y) for step in range(2, Z + 1)]
    attn_kept = [attn_part(found_at(step), 1 - other_y) for step in range(1, Z + 1)]
    attn_got[0], *attn_later = order((attn_got[0], *attn_later), (forget_term, total_down))
    attn_total = attn_kept[0].astype(f32) + attn_got[0].astype(f32)
    for step in range(1, Z):
        attn_sent = attn_total.astype(bf16)
        attn_z = along_z(attn_sent)
        if step == 1:
            heads_near, heads_far = order((heads_near, heads_far), (attn_sent,))
            grad_heads = jnp.concatenate((heads_near, heads_far), 0)
            hidden_partial = back_through_heads(grad_heads, grad_forget, weight_heads, forget_weight)
        (sent,) = order((attn_later[step - 1],), (attn_got[step - 1],))
        attn_got.append(swap(sent, "y"))
        if step == 1:
            attn_z, hidden_partial, both_scattered = order((attn_z, hidden_partial, both_scattered), (forget_got,))
            hidden_near = near_sum(hidden_partial[:far])
            hidden_x = swap(near_sum(hidden_partial[far:]).astype(bf16), "x")
            both_block = exchange(both_scattered.reshape(GROUP, rows, 2 * units), ("c", "x"))
            ffn_gate_grad, ffn_up_grad = unpack_units(both_block, unit)
        if step == 2:
            attn_z, hidden_x, hidden_near = order((attn_z, hidden_x, hidden_near), (ffn_gate_grad, layer_output))
            grad_hidden_one = hidden_near + hidden_x.astype(f32)
            normed, inv_one = row_norm(tokens)
            norm_one_partial = jnp.sum(grad_hidden_one * normed, 0)
            norm_two_partial = jnp.sum(grad_hidden_two * normed_two, 0)
            vectors = jnp.concatenate(
                (
                    norm_one_partial.reshape(devices, rows),
                    norm_two_partial.reshape(devices, rows),
                    jnp.broadcast_to(bias_sum[None], (devices, H)),
                ),
                1,
            )
            vectors_got = exchange(vectors, ALL)
            input_grad = grad_middle + norm_back(grad_hidden_one * gain_one, normed, inv_one)
        if step == 3:
            attn_z, down_scattered = order((attn_z, down_scattered), (vectors_got,))
        attn_total = attn_kept[step].astype(f32) + attn_got[step].astype(f32) + attn_z.astype(f32)
    ffn_down_grad = down_scattered.astype(f32)
    forget_got = forget_got.astype(f32).reshape(Z * size_w * 2, 2, size_r, 2, rows, LANES).sum((0, 2))
    forget_grad = forget_got[..., :LOCAL_HEADS].reshape(GROUP, rows, LOCAL_HEADS).transpose(1, 0, 2).reshape(rows, H)
    vectors_sum = jnp.sum(vectors_got, 0)
    norm_one_grad, norm_two_grad = vectors_sum[:rows], vectors_sum[rows : 2 * rows]
    forget_bias_grad = vectors_sum[2 * rows :]
    attn_sum = sum_over_rest(attn_total).astype(bf16)
    w_output_grad = transpose_quarters(attn_sum[4 * rows :]).astype(f32)
    query_grad, key_grad, value_grad, gate_out_grad = unpack_heads(
        exchange(attn_sum[: 4 * rows].reshape(4, rows, width), ("c", "x")), 4
    )
    return (
        layer_output,
        input_grad,
        norm_one_grad,
        query_grad,
        key_grad,
        value_grad,
        gate_out_grad,
        forget_grad,
        forget_bias_grad,
        w_output_grad,
        norm_two_grad,
        ffn_gate_grad,
        ffn_up_grad,
        ffn_down_grad,
    )


def solution(mesh):
    fsdp, rep = mesh.shape["fsdp"], mesh.shape["rep"]
    finer = Mesh(mesh.devices.reshape(Z, fsdp // 16, 2, 2, rep // 2, 2), ALL)
    rows, line = P(ALL, None), P(ALL)
    in_specs = (
        rows, rows, line, rows, rows, rows, rows, rows, P(), rows, line, rows, rows, rows, rows,
    )
    out_specs = (
        rows, rows, line, rows, rows, rows, rows, rows, P(), rows, line, rows, rows, rows,
    )
    return jax.shard_map(shards, mesh=finer, in_specs=in_specs, out_specs=out_specs, check_vma=False)
```

```python
import math

import jax
import jax.numpy as jnp
from jax import lax
from jax.experimental import pallas as pl
from jax.experimental.pallas import tpu as pltpu
from jax.sharding import Mesh
from jax.sharding import PartitionSpec as P

H = 24
HEAD = 64
Z = 4
GROUP = 4
LANES = 128
TILE = 256
LOCAL_HEADS = H // GROUP

epsilon = 1e-06
negative_big = -1e30
bf16 = jnp.bfloat16
f32 = jnp.float32
ALL = ("z", "w", "y", "c", "r", "x")
REST = ("w", "r")
ANY = pl.BlockSpec(memory_space=pl.ANY)
kernel_params = pltpu.CompilerParams(vmem_limit_bytes=48 * 1024 * 1024)


def row_norm(tokens):
    inverse_rms = lax.rsqrt(jnp.mean(tokens * tokens, -1, keepdims=True) + epsilon)
    return (tokens * inverse_rms, inverse_rms)


def norm_back(grad_hat, normed, inverse_rms):
    return inverse_rms * (grad_hat - normed * jnp.mean(grad_hat * normed, -1, keepdims=True))


def product(left, right):
    return jnp.dot(left, right, preferred_element_type=f32)


def product_nt(left, right, precision=None):
    return lax.dot_general(
        left, right, (((1,), (1,)), ((), ())), preferred_element_type=f32, precision=precision
    )


def product_tn(left, right, precision=None):
    return lax.dot_general(
        left, right, (((0,), (0,)), ((), ())), preferred_element_type=f32, precision=precision
    )


def place_in_ring(index):
    return index ^ (index >> 1)


def found_at(step):
    return place_in_ring((place_in_ring(lax.axis_index("z")) - step) & 3)


def along_z(block):
    return lax.ppermute(block, "z", [(0, 1), (1, 3), (3, 2), (2, 0)])


def swap(value, axis):
    return lax.ppermute(value, axis, [(0, 1), (1, 0)])


def has_rest():
    return lax.axis_size("w") * lax.axis_size("r") > 1


def over_rest(block):
    if not has_rest():
        return block[None, None]
    return lax.all_gather(lax.all_gather(block, "r"), "w")


def sum_over_rest(total):
    if not has_rest():
        return total[0, 0]
    return lax.psum_scatter(lax.psum_scatter(total, "w"), "r")


def order(values, after):
    count = len(values)
    if has_rest():
        return values
    return pl.pallas_call(
        lambda *refs: None,
        in_specs=[ANY] * (count + len(after)),
        out_specs=[ANY] * count,
        out_shape=[jax.ShapeDtypeStruct(value.shape, value.dtype) for value in values],
        input_output_aliases={at: at for at in range(count)},
        name="order",
    )(*values, *after)


def arrange(arrivals, axis, shape, reorder, spots):
    mine = lax.axis_index(axis)
    blocks = [block for _, _, block in arrivals]
    if has_rest():
        whole = jnp.zeros((Z, 2, *blocks[0].shape), blocks[0].dtype)
        for step, other, block in arrivals:
            at = (found_at(step), mine ^ other)
            whole = lax.dynamic_update_slice(whole, block[None, None], (*at, *[0] * block.ndim))
        return reorder(whole)
    blocks = [block.reshape(-1, block.shape[-1]) for block in blocks]
    places = jnp.stack([found_at(step) for step in range(Z)] + [mine, 1 - mine]).astype(jnp.int32)

    def kernel(places_ref, *refs):
        block_refs, outs, sems = refs[: len(blocks)], refs[len(blocks) : -1], refs[-1]
        copies = []
        for at, (step, other, _) in enumerate(arrivals):
            for out, first, rows, spot in spots(outs, places_ref[step], places_ref[Z + other]):
                source = block_refs[at].at[pl.ds(first, rows)]
                copies.append(pltpu.make_async_copy(source, spot, sems.at[len(copies)]))
        for copy in copies:
            copy.start()
        for copy in copies:
            copy.wait()

    return pl.pallas_call(
        kernel,
        in_specs=[pl.BlockSpec(memory_space=pltpu.SMEM)]
        + [pl.BlockSpec(memory_space=pltpu.VMEM)] * len(blocks),
        out_specs=[ANY] * len(shape),
        out_shape=[jax.ShapeDtypeStruct(one, bf16) for one in shape],
        scratch_shapes=[pltpu.SemaphoreType.DMA((8 * len(blocks),))],
        compiler_params=kernel_params,
        name="arrange",
    )(places, *blocks)


def group_gather(own, axis):
    over = swap(own, axis)
    return jnp.concatenate((own, swap(own, "c"), over, swap(over, "c")), 0)


def near_sum(partial):
    rows = partial.shape[0] // 2
    return core_sum(partial[:rows], partial[rows:])


def core_sum(own, other):
    return own.astype(f32) + swap(other, "c").astype(f32)


def group_scatter(partial, axis):
    rows = partial.shape[0] // 2
    over = swap(near_sum(partial[rows:]).astype(bf16), axis)
    return near_sum(partial[:rows]) + over.astype(f32)


def exchange(shares, axes):
    return lax.all_to_all(shares, axes, 0, 0, tiled=True)


def transpose_quarters(block):
    return lax.ppermute(
        block, ("z", "c", "x"), [(i * GROUP + j, j * GROUP + i) for i in range(Z) for j in range(GROUP)]
    )


def gather_units(block):
    if has_rest():
        block = lax.all_gather(block, "r", axis=1)
    return lax.all_gather(block.reshape(-1, block.shape[-1]), ("z", "w", "y"), axis=0, tiled=True)


def scatter_units(total, halves, rows, axes):
    if not has_rest():
        return lax.psum_scatter(total, axes, scatter_dimension=0, tiled=True)
    kept = lax.psum_scatter(total, ("z", "w", "y"), scatter_dimension=0, tiled=True)
    kept = kept.reshape(halves, -1, halves, rows, kept.shape[-1])
    return lax.psum_scatter(kept, "r", scatter_dimension=1).reshape(-1, kept.shape[-1])


def pack_heads(weights):
    rows, width = weights[0].shape
    part = width // GROUP

    def kernel(*refs):
        for at, ref in enumerate(refs[:-1]):
            for to in range(GROUP):
                refs[-1][to, :, at * part : (at + 1) * part] = ref[:, to * part : (to + 1) * part]

    return pl.pallas_call(
        kernel, out_shape=jax.ShapeDtypeStruct((GROUP, rows, len(weights) * part), bf16), name="pack_heads"
    )(*weights)


def unpack_heads(shares, count):
    rows, part = shares.shape[1], shares.shape[2] // count

    def kernel(ref, *outs):
        for at, out in enumerate(outs):
            for to in range(GROUP):
                out[:, to * part : (to + 1) * part] = ref[to, :, at * part : (at + 1) * part].astype(f32)

    whole = jax.ShapeDtypeStruct((rows, GROUP * part), f32)
    return pl.pallas_call(kernel, out_shape=[whole] * count, name="unpack_heads")(shares)


def unit_chunks(unit):
    for at in range(2 * Z):
        for place in range(GROUP):
            here = at * unit
            yield place, here // TILE * 2 * TILE + here % TILE, (at * GROUP + place) * unit


def pack_units(gate, up, unit):
    rows, hidden = gate.shape
    part = hidden // GROUP
    if has_rest():
        size = (rows, Z, lax.axis_size("w"), 2, 2, lax.axis_size("r"), 2, unit)
        both = [
            one.reshape(size).transpose(4, 6, 0, 1, 2, 3, 5, 7).reshape(GROUP, rows, part // TILE, TILE)
            for one in (gate, up)
        ]
        return jnp.stack(both, 3).reshape(GROUP, rows, 2 * part)

    def kernel(gate_ref, up_ref, out):
        for place, here, there in unit_chunks(unit):
            out[place, :, here : here + unit] = gate_ref[:, there : there + unit]
            out[place, :, here + TILE : here + TILE + unit] = up_ref[:, there : there + unit]

    return pl.pallas_call(
        kernel, out_shape=jax.ShapeDtypeStruct((GROUP, rows, 2 * part), bf16), name="pack_units"
    )(gate, up)


def unpack_units(shares, unit):
    rows, part = shares.shape[1], shares.shape[2] // 2
    if has_rest():
        size = (2, 2, rows, Z, lax.axis_size("w"), 2, lax.axis_size("r"), unit)
        both = shares.reshape(GROUP, rows, part // TILE, 2, TILE)
        return [
            both[:, :, :, at].reshape(size).transpose(2, 3, 4, 5, 0, 6, 1, 7).reshape(rows, GROUP * part).astype(f32)
            for at in range(2)
        ]

    def kernel(ref, gate_ref, up_ref):
        for place, here, there in unit_chunks(unit):
            gate_ref[:, there : there + unit] = ref[place, :, here : here + unit].astype(f32)
            up_ref[:, there : there + unit] = ref[place, :, here + TILE : here + TILE + unit].astype(f32)

    whole = jax.ShapeDtypeStruct((rows, GROUP * part), f32)
    return pl.pallas_call(kernel, out_shape=[whole, whole], name="unpack_units")(shares)


def triangle(length):
    rows = lax.broadcasted_iota(jnp.int32, (length, length), 0)
    cols = lax.broadcasted_iota(jnp.int32, (length, length), 1)
    return rows >= cols


def decays(forget_pre, tri):
    log_gate = jax.nn.log_sigmoid(forget_pre)
    highest = lax.Precision.HIGHEST
    down = jnp.dot(tri, log_gate, preferred_element_type=f32, precision=highest)
    across = lax.dot_general(
        log_gate, tri, (((0,), (1,)), ((), ())), preferred_element_type=f32, precision=highest
    )
    return down, across


def half_mask(half):
    lane = lax.broadcasted_iota(jnp.int32, (1, LANES), 1)
    return (lane >= HEAD) == bool(half)


def attend_kernel(q_ref, k_ref, v_ref, gate_ref, forget_ref, seg_col, seg_row, gated_ref, attended_ref, log_ref):
    length = q_ref.shape[0]
    causal = triangle(length)
    down, across = decays(forget_ref[...], causal.astype(f32))
    bias = jnp.where(causal & (seg_col[...] == seg_row[0]), 0.0, negative_big)
    lane = lax.broadcasted_iota(jnp.int32, (length, LANES), 1)
    logs = jnp.zeros((length, LANES), f32)
    for pair in range(LOCAL_HEADS // 2):
        cols = slice(pair * LANES, (pair + 1) * LANES)
        query, key, value = q_ref[:, cols], k_ref[:, cols], v_ref[:, cols].astype(bf16)
        both = []
        for half in range(2):
            head = 2 * pair + half
            mine = half_mask(half)
            scaled = jnp.where(mine, query, 0) * jnp.asarray(0.125, bf16)
            scores = product_nt(scaled, key) + down[:, head : head + 1] - across[head : head + 1, :] + bias
            top = jnp.max(scores, -1, keepdims=True)
            shifted = jnp.exp(scores - top)
            total = jnp.sum(shifted, -1, keepdims=True)
            probs = (shifted * (1.0 / total)).astype(bf16)
            both.append(jnp.where(mine, product(probs, value), 0.0))
            logs = jnp.where(lane == head, top + jnp.log(total), logs)
        attended = both[0] + both[1]
        attended_ref[:, cols] = attended
        gated_ref[:, cols] = (attended * jax.nn.sigmoid(gate_ref[:, cols])).astype(bf16)
    log_ref[...] = logs


def attend_back_kernel(
    q_ref, k_ref, v_ref, gate_ref, forget_ref, seg_col, seg_row, attended_ref, log_ref, grad_ref, heads_ref, dforget_ref,
):
    length, width = q_ref.shape
    causal = triangle(length)
    tri = causal.astype(f32)
    down, across = decays(forget_ref[...], tri)
    bias = jnp.where(causal & (seg_col[...] == seg_row[0]), 0.0, negative_big)
    lane = lax.broadcasted_iota(jnp.int32, (length, LANES), 1)
    grad_decay = jnp.zeros((length, LANES), f32)
    for pair in range(LOCAL_HEADS // 2):
        cols = slice(pair * LANES, (pair + 1) * LANES)
        query, key, value = q_ref[:, cols], k_ref[:, cols], v_ref[:, cols].astype(bf16)
        out_gate = jax.nn.sigmoid(gate_ref[:, cols])
        grad_gated = grad_ref[:, cols]
        grad_att = (grad_gated * out_gate).astype(bf16)
        grad_gate = (grad_gated * attended_ref[:, cols] * out_gate * (1.0 - out_gate)).astype(bf16)
        dq, dk, dv = [], [], []
        for half in range(2):
            head = 2 * pair + half
            mine = half_mask(half)
            scaled = jnp.where(mine, query, 0) * jnp.asarray(0.125, bf16)
            scores = product_nt(scaled, key) + down[:, head : head + 1] - across[head : head + 1, :] + bias
            probs = jnp.exp(scores - log_ref[:, head : head + 1])
            grad_prob = product_nt(jnp.where(mine, grad_att, 0), value)
            delta = jnp.sum(probs * grad_prob, -1, keepdims=True)
            grad_scores = (probs * (grad_prob - delta)).astype(bf16)
            dq.append(product(grad_scores, key))
            dk.append(product_tn(grad_scores, query))
            dv.append(product_tn(probs.astype(bf16), grad_att))
            one = (lane == head).astype(bf16)
            grad_decay = grad_decay + product(grad_scores, one) - product_tn(grad_scores, one)
        first = half_mask(0)
        found = (
            (jnp.where(first, dq[0], dq[1]) * 0.125).astype(bf16),
            (jnp.where(first, dk[0], dk[1]) * 0.125).astype(bf16),
            jnp.where(first, dv[0], dv[1]).astype(bf16),
            grad_gate,
        )
        for at, one in enumerate(found):
            heads_ref[:, at * width + pair * LANES : at * width + (pair + 1) * LANES] = one
    later = product_tn(tri, grad_decay, lax.Precision.HIGHEST)
    dforget_ref[...] = (later * jax.nn.sigmoid(-forget_ref[...])).astype(bf16)


def attention_specs(length, width, first):
    def columns(at):
        return pl.BlockSpec((length, width), lambda i: (first + i, at))

    lanes = pl.BlockSpec((length, LANES), lambda i: (first + i, 0))
    seg_col = pl.BlockSpec((length, 1), lambda i: (first + i, 0))
    seg_row = pl.BlockSpec((1, 1, length), lambda i: (first + i, 0, 0))
    return columns, lanes, seg_col, seg_row


def attend(query_key, value_gate, forget_pre, seg_col, seg_row, length):
    tokens, width = query_key.shape[0], query_key.shape[1] // 2
    columns, lanes, col_spec, row_spec = attention_specs(length, width, 0)
    return pl.pallas_call(
        attend_kernel,
        grid=(tokens // length,),
        in_specs=[columns(0), columns(1), columns(0), columns(1), lanes, col_spec, row_spec],
        out_specs=[columns(0), columns(0), lanes],
        out_shape=[
            jax.ShapeDtypeStruct((tokens, width), bf16),
            jax.ShapeDtypeStruct((tokens, width), f32),
            jax.ShapeDtypeStruct((tokens, LANES), f32),
        ],
        compiler_params=kernel_params,
        cost_estimate=pl.CostEstimate(
            flops=4 * tokens * length * width, bytes_accessed=14 * tokens * width, transcendentals=0
        ),
        name="attend",
    )(query_key, query_key, value_gate, value_gate, forget_pre, seg_col, seg_row)


def attend_back(query_key, value_gate, forget_pre, seg_col, seg_row, attended, logs, grad_gated, length, first):
    tokens, width = grad_gated.shape
    columns, lanes, col_spec, row_spec = attention_specs(length, width, first)
    own_columns, own_lanes, _, _ = attention_specs(length, width, 0)
    return pl.pallas_call(
        attend_back_kernel,
        grid=(tokens // length,),
        in_specs=[
            columns(0), columns(1), columns(0), columns(1), lanes, col_spec, row_spec,
            columns(0), lanes, own_columns(0),
        ],
        out_specs=[pl.BlockSpec((length, 4 * width), lambda i: (i, 0)), own_lanes],
        out_shape=[
            jax.ShapeDtypeStruct((tokens, 4 * width), bf16),
            jax.ShapeDtypeStruct((tokens, LANES), bf16),
        ],
        compiler_params=kernel_params,
        cost_estimate=pl.CostEstimate(
            flops=0, bytes_accessed=0, transcendentals=0
        ),
        name="attend_back",
    )(query_key, query_key, value_gate, value_gate, forget_pre, seg_col, seg_row, attended, logs, grad_gated)


def attn_terms(hidden, grad_heads, gated, grad_branch, down_term, rows):
    unit = down_term.shape[0] // (2 * Z)
    tokens, width = hidden.shape
    part, half = gated.shape[1], tokens // 2

    def both(left_ref, right_refs):
        near = product_tn(left_ref[:half, :], right_refs[0][...])
        return (near + product_tn(left_ref[half:, :], right_refs[1][...])).astype(bf16)

    def kernel(hidden_ref, near_ref, far_ref, gated_ref, branch_near, branch_far, down_ref, out_ref, out_term):
        at_z = pl.program_id(0)

        @pl.when(at_z == 0)
        def _():
            out_term[...] = both(gated_ref, (branch_near, branch_far))

        term = both(hidden_ref, (near_ref, far_ref))
        for at_y in range(2):
            out_ref[at_y, : 4 * rows] = term[at_y * 4 * rows : (at_y + 1) * 4 * rows]
            first = pl.multiple_of((at_y * 4 + at_z) * rows, rows)
            out_ref[at_y, 4 * rows : 5 * rows] = out_term[pl.ds(first, rows), :]
            out_ref[at_y, 5 * rows :] = down_ref[at_y * unit : (at_y + 1) * unit]

    piece = pl.BlockSpec((half, width), lambda z: (0, 0))
    return pl.pallas_call(
        kernel,
        grid=(Z,),
        in_specs=[
            pl.BlockSpec((tokens, 8 * rows), lambda z: (0, z)),
            piece,
            piece,
            pl.BlockSpec((tokens, part), lambda z: (0, 0)),
            piece,
            piece,
            pl.BlockSpec((2 * unit, width), lambda z: (z, 0)),
        ],
        out_specs=pl.BlockSpec((2, 5 * rows + unit, width), lambda z: (z, 0, 0)),
        out_shape=jax.ShapeDtypeStruct((2 * Z, 5 * rows + unit, width), bf16),
        scratch_shapes=[pltpu.VMEM((part, width), bf16)],
        compiler_params=kernel_params,
        cost_estimate=pl.CostEstimate(
            flops=2 * tokens * width * (width + part), bytes_accessed=10 * tokens * width, transcendentals=0
        ),
        name="attn_terms",
    )(hidden, *grad_heads, gated, *grad_branch, down_term)


def back_through_heads(grad_heads, grad_forget, weight_heads, forget_weight):
    tokens, width = grad_heads.shape
    tile, rows = width // 4, tokens // GROUP

    def kernel(heads_ref, forget_ref, weight_ref, forget_weight_ref, *outs):
        total = product_nt(heads_ref[...], weight_ref[...]) + product_nt(forget_ref[...], forget_weight_ref[...])
        for at, out in enumerate(outs):
            out[...] = total[at * rows : (at + 1) * rows].astype(bf16)

    return pl.pallas_call(
        kernel,
        grid=(4,),
        in_specs=[
            pl.BlockSpec((tokens, width), lambda j: (0, 0)),
            pl.BlockSpec((tokens, LANES), lambda j: (0, 0)),
            pl.BlockSpec((tile, width), lambda j: (j, 0)),
            pl.BlockSpec((tile, LANES), lambda j: (j, 0)),
        ],
        out_specs=[pl.BlockSpec((rows, tile), lambda j: (0, j))] * GROUP,
        out_shape=[jax.ShapeDtypeStruct((rows, width), bf16)] * GROUP,
        compiler_params=kernel_params,
        cost_estimate=pl.CostEstimate(
            flops=2 * tokens * width * width, bytes_accessed=8 * tokens * width, transcendentals=0
        ),
        name="back_through_heads",
    )(grad_heads, grad_forget, weight_heads, forget_weight)


def ffn_tile(hidden_ref, out_grad_ref, both_ref, down_ref, act_ref, dboth_ref):
    both = product(hidden_ref[...], both_ref[...])
    gate_ffn, up_ffn = both[:, :TILE], both[:, TILE:]
    grad_act = product_nt(out_grad_ref[...], down_ref[...])
    sigmoid_gate = jax.nn.sigmoid(gate_ffn)
    silu = gate_ffn * sigmoid_gate
    act_ref[...] = (silu * up_ffn).astype(bf16)
    grad_gate = grad_act * up_ffn * sigmoid_gate * (1.0 + gate_ffn * (1.0 - sigmoid_gate))
    dboth_ref[:, :TILE] = grad_gate.astype(bf16)
    dboth_ref[:, TILE:] = (grad_act * silu).astype(bf16)


def feed_forward(parts, out_grad, weight_both, weight_down):
    tokens, width = out_grad.shape
    units = weight_down.shape[0]
    steps = units // TILE
    whole = pl.BlockSpec((tokens, width), lambda j: (0, 0))
    rows = tokens // GROUP

    def kernel(*refs):
        joined = refs[GROUP + 3]

        @pl.when(pl.program_id(0) == 0)
        def _():
            for at in range(GROUP):
                joined[at * rows : (at + 1) * rows, :] = refs[at][...]

        ffn_tile(joined, *refs[GROUP : GROUP + 3], *refs[GROUP + 4 :])

    first = pl.BlockSpec((rows, width), lambda j: (0, 0))
    return pl.pallas_call(
        kernel,
        grid=(steps,),
        in_specs=[first] * GROUP
        + [
            whole,
            pl.BlockSpec((width, 2 * TILE), lambda j: (0, j)),
            pl.BlockSpec((TILE, width), lambda j: (j, 0)),
        ],
        out_specs=[
            whole,
            pl.BlockSpec((tokens, TILE), lambda j: (0, j)),
            pl.BlockSpec((tokens, 2 * TILE), lambda j: (0, j)),
        ],
        out_shape=[
            jax.ShapeDtypeStruct((tokens, width), bf16),
            jax.ShapeDtypeStruct((tokens, units), bf16),
            jax.ShapeDtypeStruct((tokens, 2 * units), bf16),
        ],
        compiler_params=kernel_params,
        cost_estimate=pl.CostEstimate(
            flops=6 * tokens * width * units, bytes_accessed=12 * tokens * width, transcendentals=0
        ),
        name="feed_forward",
    )(*parts, out_grad, weight_both, weight_down)


def shards(
    inputs,
    segment_ids,
    norm_one,
    w_query,
    w_key,
    w_value,
    w_gate_out,
    w_forget,
    forget_bias,
    w_output,
    norm_two,
    w_ffn_gate,
    w_ffn_up,
    w_ffn_down,
    out_grad,
):
    length, width = inputs.shape
    rows, unit = norm_one.shape[0], w_ffn_down.shape[0]
    size_w, size_r = lax.axis_size("w"), lax.axis_size("r")
    devices = math.prod(lax.axis_size(axis) for axis in ALL)
    place = lax.axis_index("c") * 2 + lax.axis_index("x")
    part = width // GROUP
    units = w_ffn_gate.shape[1] // GROUP
    far = 2 * length
    alone = not has_rest()

    heads_block = exchange(pack_heads((w_query, w_key, w_value, w_gate_out)), ("c", "x"))
    output_block = transpose_quarters(w_output)
    (units_shares,) = order((pack_units(w_ffn_gate, w_ffn_up, unit),), (heads_block,))
    units_block = exchange(units_shares, ("c", "x"))

    attn = [jnp.concatenate((over_rest(heads_block.reshape(4 * rows, width)), over_rest(output_block)), 2)]
    both = [units_block.reshape(4 * rows, 2 * units)]
    if alone:
        down_y = swap(w_ffn_down, "y")
        first = lax.axis_index("y") == 0
        down_pair = jnp.concatenate((jnp.where(first, w_ffn_down, down_y), jnp.where(first, down_y, w_ffn_down)), 0)
    else:
        down_pair = w_ffn_down
    (inputs_sent,) = order((inputs,), (heads_block, down_pair))
    inputs_x = swap(inputs_sent, "x")
    attn_y = [swap(attn[0], "y")]
    attn.append(along_z(attn[0]))

    (attn[1],) = order((attn[1],), (attn_y[0],))
    attn_y.append(swap(attn[1], "y"))
    attn.append(along_z(attn[1]))

    attn[2], out_grad_sent, down_pair = order((attn[2], out_grad, down_pair), (attn_y[1], inputs_x))
    out_grad_x = swap(out_grad_sent, "x")
    attn_y.append(swap(attn[2], "y"))
    attn.append(along_z(attn[2]))

    small = jnp.concatenate(
        (w_forget, norm_one[:, None], norm_two[:, None], jnp.zeros((rows, LANES - H - 2), bf16)), 1
    )
    (small,) = order((small,), (units_block,))
    seg_rows = length // LANES
    seg_own = jnp.pad(segment_ids.astype(bf16).reshape(seg_rows, LANES), ((0, 16 - seg_rows), (0, 0)))
    small = jnp.concatenate((small, seg_own), 0)
    small = exchange(jnp.broadcast_to(small[None], (devices, rows + 16, LANES)), ALL)
    small = small.reshape(devices, rows + 16, LANES)
    members = small[:, rows : rows + seg_rows].reshape(Z, size_w, 2, 2, size_r, 2, seg_rows, LANES)

    def member(other_x, other_c):
        at = [lax.axis_index(axis) for axis in ALL]
        at[5], at[3] = at[5] ^ other_x, at[3] ^ other_c
        return lax.dynamic_slice(members, (*at, 0, 0), (1, 1, 1, 1, 1, 1, seg_rows, LANES)).reshape(1, length)

    seg_all = jnp.concatenate((member(0, 0), member(0, 1), member(1, 0), member(1, 1)), 0).astype(f32)
    seg_col, seg_row = seg_all.reshape(-1, 1), seg_all[:, None, :]
    small = small[:, :rows].reshape(width, LANES)
    gain_one, gain_two = small[:, H].astype(f32), small[:, H + 1].astype(f32)
    forget_weight = lax.dynamic_slice(small, (0, place * LOCAL_HEADS), (width, LOCAL_HEADS))
    forget_weight = jnp.pad(forget_weight, ((0, 0), (0, LANES - LOCAL_HEADS)))
    bias_part = lax.dynamic_slice(forget_bias, (place * LOCAL_HEADS,), (LOCAL_HEADS,)).astype(f32)
    bias_part = jnp.pad(bias_part, (0, LANES - LOCAL_HEADS))

    attn[3], both[0] = order((attn[3], both[0]), (attn_y[2],))
    attn_y.append(swap(attn[3], "y"))
    both.append(along_z(both[0]))
    if alone:
        weight_down = lax.all_gather(down_pair, "z", axis=0, tiled=True)
    else:
        weight_down = gather_units(down_pair.reshape(1, 1, unit, width))

    def attn_order(whole):
        heads = whole[:, :, :, :, : 4 * rows].reshape(Z, 2, size_w, size_r, 2, 2, rows, width)
        out = whole[:, :, :, :, 4 * rows :].reshape(2, 2, 2, size_w, size_r, rows, width)
        return (
            heads.transpose(0, 2, 1, 4, 3, 5, 6, 7).reshape(width, width),
            out.transpose(3, 2, 0, 4, 1, 5, 6).reshape(part, width),
        )

    def attn_spots(outs, at_z, at_y):
        first = pl.multiple_of((at_z * 2 + at_y) * 4 * rows, 4 * rows)
        yield outs[0], 0, 4 * rows, outs[0].at[pl.ds(first, 4 * rows)]
        yield outs[1], 4 * rows, rows, outs[1].at[pl.ds(pl.multiple_of((at_y * 4 + at_z) * rows, rows), rows)]

    arrivals = [(step, other, (attn, attn_y)[other][step]) for step in range(Z) for other in range(2)]
    weight_heads, weight_out = arrange(arrivals, "y", ((width, width), (part, width)), attn_order, attn_spots)

    inputs_all = jnp.concatenate((inputs, swap(inputs, "c"), inputs_x, swap(inputs_x, "c")), 0)
    out_grad_all = jnp.concatenate((out_grad, swap(out_grad, "c"), out_grad_x, swap(out_grad_x, "c")), 0)
    hidden_one = (row_norm(inputs_all.astype(f32))[0] * gain_one).astype(bf16)

    hidden_one, both[0], both[1] = order((hidden_one, both[0], both[1]), (weight_out, out_grad_x))
    both_y = [None] * Z
    both_y[1] = swap(both[1], "y")
    both.append(along_z(both[1]))
    both_y[0] = swap(both[0], "y")
    query_key = product(hidden_one, weight_heads[:, : 2 * part]).astype(bf16)
    value_gate = product(hidden_one, weight_heads[:, 2 * part :])
    forget_pre = product(hidden_one, forget_weight) + bias_part
    gated_att, attended, logs = attend(query_key, value_gate, forget_pre, seg_col, seg_row, length)
    partial = product(gated_att, weight_out).astype(bf16)

    partial, both[2] = order((partial, both[2]), (both_y[1], out_grad_all))
    both_y[2] = swap(both[2], "y")
    both.append(along_z(both[2]))
    branch_x = swap(near_sum(partial[far:]).astype(bf16), "x")
    branch_near = near_sum(partial[:far])

    branch_x, branch_near, both[3] = order((branch_x, branch_near, both[3]), (both_y[0], both_y[2]))
    both_y[3] = swap(both[3], "y")
    tokens = inputs.astype(f32)
    middle = tokens + (branch_near + branch_x.astype(f32))
    normed_two, inv_two = row_norm(middle)
    hidden_own = (normed_two * gain_two).astype(bf16)
    hidden_x = swap(hidden_own, "x")
    hidden_parts = (hidden_own, swap(hidden_own, "c"), hidden_x, swap(hidden_x, "c"))
    if not alone:
        weight_both = gather_units(both[0].reshape(2, 2, rows, 2 * units))
    else:

        def both_spots(outs, at_z, at_y):
            first = pl.multiple_of((at_z * 2 + at_y) * 4 * rows, 4 * rows)
            yield outs[0], 0, 4 * rows, outs[0].at[pl.ds(first, 4 * rows)]

        arrivals = [(step, other, (both, both_y)[other][step]) for step in range(Z) for other in range(2)]
        (weight_both,) = arrange(arrivals, "y", ((width, 2 * units),), None, both_spots)

    hidden_two, activation, grad_both = feed_forward(hidden_parts, out_grad_all, weight_both, weight_down)
    both_term = product_tn(hidden_two, grad_both).astype(bf16)
    grad_both, activation = order((grad_both, activation), (both_term,))
    both_scattered = scatter_units(both_term, 2, rows, ("z", "y"))
    grad_hidden = product_nt(grad_both, weight_both).astype(bf16)
    near_sent = near_sum(grad_hidden[far:]).astype(bf16)
    grad_hidden_x = swap(near_sent, "x")
    near_own = near_sum(grad_hidden[:far])
    (activation,) = order((activation,), (near_sent,))
    down_term = product_tn(activation, out_grad_all).astype(bf16)
    layer_partial = product(activation, weight_down).astype(bf16)
    grad_hidden_x, near_own = order((grad_hidden_x, near_own), (layer_partial, down_term))

    grad_hidden_two = near_own + grad_hidden_x.astype(f32)
    grad_middle = out_grad.astype(f32) + norm_back(grad_hidden_two * gain_two, normed_two, inv_two)
    grad_own = grad_middle.astype(bf16)
    grad_c = swap(grad_own, "c")
    grad_x = swap(grad_own, "x")

    grad_near = jnp.concatenate((grad_own, grad_c), 0)

    def back(grad_branch, first):
        return attend_back(
            query_key, value_gate, forget_pre, seg_col, seg_row,
            attended, logs, product_nt(grad_branch, weight_out), length, first,
        )

    heads_near, forget_near = back(grad_near, 0)
    grad_x, heads_near, layer_partial = order((grad_x, heads_near, layer_partial), ())
    layer_x = swap(near_sum(layer_partial[far:]).astype(bf16), "x")
    layer_near = near_sum(layer_partial[:far])
    grad_far = jnp.concatenate((grad_x, swap(grad_x, "c")), 0)
    heads_far, forget_far = back(grad_far, 2)
    if not alone:
        down_scattered = scatter_units(down_term, 1, unit, ("z",))
    if alone:
        terms = [attn_terms(
            hidden_one, (heads_near, heads_far), gated_att, (grad_near, grad_far), down_term, rows
        )]

        def attn_part(at_z, at_y):
            return lax.dynamic_index_in_dim(terms[-1], at_z * 2 + at_y, 0)[None]

    else:
        grad_heads = jnp.concatenate((heads_near, heads_far), 0)
        grad_branch = jnp.concatenate((grad_near, grad_far), 0)
        heads_term = product_tn(hidden_one, grad_heads).astype(bf16)
        out_term = product_tn(gated_att, grad_branch).astype(bf16)

        def attn_part(at_z, at_y):
            heads = heads_term.reshape(Z, size_w, 2, 2, size_r, 2, rows, width)
            size = (1, size_w, 1, 2, size_r, 2, rows, width)
            heads = lax.dynamic_slice(heads, (at_z, 0, at_y, 0, 0, 0, 0, 0), size)
            heads = heads[0, :, 0].transpose(0, 2, 1, 3, 4, 5).reshape(size_w, size_r, 4 * rows, width)
            out = out_term.reshape(size_w, 2, 2, size_r, 2, rows, width)
            size = (size_w, 1, 1, size_r, 1, rows, width)
            out = lax.dynamic_slice(out, (0, at_y, at_z // 2, 0, at_z % 2, 0, 0), size)
            return jnp.concatenate((heads, out.reshape(size_w, size_r, rows, width)), 2)

    other_y = 1 - lax.axis_index("y")
    attn_sent = attn_part(found_at(1), other_y)
    attn_got = [swap(attn_sent, "y")]
    heads_near, heads_far, forget_near, forget_far = order(
        (heads_near, heads_far, forget_near, forget_far), (attn_sent,)
    )
    if alone:
        terms += order((terms[0],), (attn_sent,))
    grad_forget = jnp.concatenate((forget_near, forget_far), 0)
    forget_term = product_tn(grad_forget, hidden_one)[:8].reshape(8, devices, rows).transpose(1, 0, 2)
    forget_got = exchange(forget_term, ALL)
    bias_sum = jnp.sum(grad_forget.astype(f32), 0)[:LOCAL_HEADS]
    bias_sum = lax.dynamic_update_slice(jnp.zeros((H,), f32), bias_sum, (place * LOCAL_HEADS,))
    attn_later = [attn_part(found_at(step), other_y) for step in range(2, Z + 1)]
    attn_kept = [attn_part(found_at(step), 1 - other_y) for step in range(1, Z + 1)]
    attn_got[0], *attn_later = order((attn_got[0], *attn_later), (forget_term, layer_x))
    attn_total = attn_kept[0].astype(f32) + attn_got[0].astype(f32)
    for step in range(1, Z):
        attn_sent = attn_total.astype(bf16)
        attn_z = along_z(attn_sent)
        if step == 1:
            heads_near, heads_far = order((heads_near, heads_far), (attn_sent,))
            grad_heads = jnp.concatenate((heads_near, heads_far), 0)
            hidden_partial = back_through_heads(grad_heads, grad_forget, weight_heads, forget_weight)
        (sent,) = order((attn_later[step - 1],), (attn_got[step - 1],))
        attn_got.append(swap(sent, "y"))
        if step == 1:
            attn_z, both_scattered, *hidden_partial = order((attn_z, both_scattered, *hidden_partial), (forget_got,))
            hidden_near = core_sum(hidden_partial[0], hidden_partial[1])
            hidden_x = swap(core_sum(hidden_partial[2], hidden_partial[3]).astype(bf16), "x")
            both_block = exchange(both_scattered.reshape(GROUP, rows, 2 * units), ("c", "x"))
            ffn_gate_grad, ffn_up_grad = unpack_units(both_block, unit)
        if step == 2:
            attn_z, hidden_near = order((attn_z, hidden_near), (layer_x,))
            grad_hidden_one = hidden_near + hidden_x.astype(f32)
            normed, inv_one = row_norm(tokens)
            norm_one_partial = jnp.sum(grad_hidden_one * normed, 0)
            norm_two_partial = jnp.sum(grad_hidden_two * normed_two, 0)
            vectors = jnp.concatenate(
                (
                    norm_one_partial.reshape(devices, rows),
                    norm_two_partial.reshape(devices, rows),
                    jnp.broadcast_to(bias_sum[None], (devices, H)),
                ),
                1,
            )
            vectors_got = exchange(vectors, ALL)
            input_grad = grad_middle + norm_back(grad_hidden_one * gain_one, normed, inv_one)
        if step == 3:
            (attn_z,) = order((attn_z,), (vectors_got, ffn_gate_grad))
            layer_output = (middle + (layer_near + layer_x.astype(f32))).astype(bf16)
        attn_total = attn_kept[step].astype(f32) + attn_got[step].astype(f32) + attn_z.astype(f32)
    forget_got = forget_got.reshape(Z * size_w * 2, 2, size_r, 2, 8, rows).sum((0, 2))
    forget_grad = forget_got[:, :, :LOCAL_HEADS].reshape(H, rows).T
    vectors_sum = jnp.sum(vectors_got, 0)
    norm_one_grad, norm_two_grad = vectors_sum[:rows], vectors_sum[rows : 2 * rows]
    forget_bias_grad = vectors_sum[2 * rows :]
    if alone:
        ffn_down_grad = attn_total[0, 0, 5 * rows :]
        attn_sum = attn_total[0, 0, : 5 * rows].astype(bf16)
    else:
        ffn_down_grad = down_scattered.astype(f32)
        attn_sum = sum_over_rest(attn_total).astype(bf16)
    w_output_grad = transpose_quarters(attn_sum[4 * rows :]).astype(f32)
    query_grad, key_grad, value_grad, gate_out_grad = unpack_heads(
        exchange(attn_sum[: 4 * rows].reshape(4, rows, width), ("c", "x")), 4
    )
    return (
        layer_output,
        input_grad,
        norm_one_grad,
        query_grad,
        key_grad,
        value_grad,
        gate_out_grad,
        forget_grad,
        forget_bias_grad,
        w_output_grad,
        norm_two_grad,
        ffn_gate_grad,
        ffn_up_grad,
        ffn_down_grad,
    )


def solution(mesh):
    fsdp, rep = mesh.shape["fsdp"], mesh.shape["rep"]
    finer = Mesh(mesh.devices.reshape(Z, fsdp // 16, 2, 2, rep // 2, 2), ALL)
    rows, line = P(ALL, None), P(ALL)
    in_specs = (
        rows, rows, line, rows, rows, rows, rows, rows, P(), rows, line, rows, rows, rows, rows,
    )
    out_specs = (
        rows, rows, line, rows, rows, rows, rows, rows, P(), rows, line, rows, rows, rows,
    )
    return jax.shard_map(shards, mesh=finer, in_specs=in_specs, out_specs=out_specs, check_vma=False)
```

```python
import math

import jax
import jax.numpy as jnp
from jax import lax
from jax.experimental import pallas as pl
from jax.experimental.pallas import tpu as pltpu
from jax.sharding import Mesh
from jax.sharding import PartitionSpec as P

H = 24
HEAD = 64
Z = 4
GROUP = 4
LANES = 128
TILE = 256
LOCAL_HEADS = H // GROUP

epsilon = 1e-06
negative_big = -1e30
bf16 = jnp.bfloat16
f32 = jnp.float32
ALL = ("z", "w", "y", "c", "r", "x")
REST = ("w", "r")
ANY = pl.BlockSpec(memory_space=pl.ANY)
kernel_params = pltpu.CompilerParams(vmem_limit_bytes=48 * 1024 * 1024)


def row_norm(tokens):
    inverse_rms = lax.rsqrt(jnp.mean(tokens * tokens, -1, keepdims=True) + epsilon)
    return (tokens * inverse_rms, inverse_rms)


def norm_back(grad_hat, normed, inverse_rms):
    return inverse_rms * (grad_hat - normed * jnp.mean(grad_hat * normed, -1, keepdims=True))


def product(left, right):
    return jnp.dot(left, right, preferred_element_type=f32)


def product_nt(left, right, precision=None):
    return lax.dot_general(
        left, right, (((1,), (1,)), ((), ())), preferred_element_type=f32, precision=precision
    )


def product_tn(left, right, precision=None):
    return lax.dot_general(
        left, right, (((0,), (0,)), ((), ())), preferred_element_type=f32, precision=precision
    )


def place_in_ring(index):
    return index ^ (index >> 1)


def found_at(step):
    return place_in_ring((place_in_ring(lax.axis_index("z")) - step) & 3)


def along_z(block):
    return lax.ppermute(block, "z", [(0, 1), (1, 3), (3, 2), (2, 0)])


def swap(value, axis):
    return lax.ppermute(value, axis, [(0, 1), (1, 0)])


def has_rest():
    return lax.axis_size("w") * lax.axis_size("r") > 1


def over_rest(block):
    if not has_rest():
        return block[None, None]
    return lax.all_gather(lax.all_gather(block, "r"), "w")


def sum_over_rest(total):
    if not has_rest():
        return total[0, 0]
    return lax.psum_scatter(lax.psum_scatter(total, "w"), "r")


def order(values, after):
    count = len(values)
    if has_rest():
        return values
    return pl.pallas_call(
        lambda *refs: None,
        in_specs=[ANY] * (count + len(after)),
        out_specs=[ANY] * count,
        out_shape=[jax.ShapeDtypeStruct(value.shape, value.dtype) for value in values],
        input_output_aliases={at: at for at in range(count)},
        name="order",
    )(*values, *after)


def arrange(arrivals, axis, shape, reorder, spots):
    mine = lax.axis_index(axis)
    blocks = [block for _, _, block in arrivals]
    if has_rest():
        whole = jnp.zeros((Z, 2, *blocks[0].shape), blocks[0].dtype)
        for step, other, block in arrivals:
            at = (found_at(step), mine ^ other)
            whole = lax.dynamic_update_slice(whole, block[None, None], (*at, *[0] * block.ndim))
        return reorder(whole)
    blocks = [block.reshape(-1, block.shape[-1]) for block in blocks]
    places = jnp.stack([found_at(step) for step in range(Z)] + [mine, 1 - mine]).astype(jnp.int32)

    def kernel(places_ref, *refs):
        block_refs, outs, sems = refs[: len(blocks)], refs[len(blocks) : -1], refs[-1]
        copies = []
        for at, (step, other, _) in enumerate(arrivals):
            for out, first, rows, spot in spots(outs, places_ref[step], places_ref[Z + other]):
                source = block_refs[at].at[pl.ds(first, rows)]
                copies.append(pltpu.make_async_copy(source, spot, sems.at[len(copies)]))
        for copy in copies:
            copy.start()
        for copy in copies:
            copy.wait()

    return pl.pallas_call(
        kernel,
        in_specs=[pl.BlockSpec(memory_space=pltpu.SMEM)]
        + [pl.BlockSpec(memory_space=pltpu.VMEM)] * len(blocks),
        out_specs=[ANY] * len(shape),
        out_shape=[jax.ShapeDtypeStruct(one, bf16) for one in shape],
        scratch_shapes=[pltpu.SemaphoreType.DMA((8 * len(blocks),))],
        compiler_params=kernel_params,
        name="arrange",
    )(places, *blocks)


def group_gather(own, axis):
    over = swap(own, axis)
    return jnp.concatenate((own, swap(own, "c"), over, swap(over, "c")), 0)


def near_sum(partial):
    rows = partial.shape[0] // 2
    return core_sum(partial[:rows], partial[rows:])


def core_sum(own, other):
    return own.astype(f32) + swap(other, "c").astype(f32)


def group_scatter(partial, axis):
    rows = partial.shape[0] // 2
    over = swap(near_sum(partial[rows:]).astype(bf16), axis)
    return near_sum(partial[:rows]) + over.astype(f32)


def exchange(shares, axes):
    return lax.all_to_all(shares, axes, 0, 0, tiled=True)


def transpose_quarters(block):
    return lax.ppermute(
        block, ("z", "c", "x"), [(i * GROUP + j, j * GROUP + i) for i in range(Z) for j in range(GROUP)]
    )


def gather_units(block):
    if has_rest():
        block = lax.all_gather(block, "r", axis=1)
    return lax.all_gather(block.reshape(-1, block.shape[-1]), ("z", "w", "y"), axis=0, tiled=True)


def scatter_units(total, halves, rows, axes):
    if not has_rest():
        return lax.psum_scatter(total, axes, scatter_dimension=0, tiled=True)
    kept = lax.psum_scatter(total, ("z", "w", "y"), scatter_dimension=0, tiled=True)
    kept = kept.reshape(halves, -1, halves, rows, kept.shape[-1])
    return lax.psum_scatter(kept, "r", scatter_dimension=1).reshape(-1, kept.shape[-1])


def pack_heads(weights):
    rows, width = weights[0].shape
    part = width // GROUP

    def kernel(*refs):
        for at, ref in enumerate(refs[:-1]):
            for to in range(GROUP):
                refs[-1][to, :, at * part : (at + 1) * part] = ref[:, to * part : (to + 1) * part]

    return pl.pallas_call(
        kernel, out_shape=jax.ShapeDtypeStruct((GROUP, rows, len(weights) * part), bf16), name="pack_heads"
    )(*weights)


def unpack_heads(shares, count):
    rows, part = shares.shape[1], shares.shape[2] // count

    def kernel(ref, *outs):
        for at, out in enumerate(outs):
            for to in range(GROUP):
                out[:, to * part : (to + 1) * part] = ref[to, :, at * part : (at + 1) * part].astype(f32)

    whole = jax.ShapeDtypeStruct((rows, GROUP * part), f32)
    return pl.pallas_call(kernel, out_shape=[whole] * count, name="unpack_heads")(shares)


def unit_chunks(unit):
    for at in range(2 * Z):
        for place in range(GROUP):
            here = at * unit
            yield place, here // TILE * 2 * TILE + here % TILE, (at * GROUP + place) * unit


def pack_units(gate, up, unit):
    rows, hidden = gate.shape
    part = hidden // GROUP
    if has_rest():
        size = (rows, Z, lax.axis_size("w"), 2, 2, lax.axis_size("r"), 2, unit)
        both = [
            one.reshape(size).transpose(4, 6, 0, 1, 2, 3, 5, 7).reshape(GROUP, rows, part // TILE, TILE)
            for one in (gate, up)
        ]
        return jnp.stack(both, 3).reshape(GROUP, rows, 2 * part)

    def kernel(gate_ref, up_ref, out):
        for place, here, there in unit_chunks(unit):
            out[place, :, here : here + unit] = gate_ref[:, there : there + unit]
            out[place, :, here + TILE : here + TILE + unit] = up_ref[:, there : there + unit]

    return pl.pallas_call(
        kernel, out_shape=jax.ShapeDtypeStruct((GROUP, rows, 2 * part), bf16), name="pack_units"
    )(gate, up)


def unpack_units(shares, unit):
    rows, part = shares.shape[1], shares.shape[2] // 2
    if has_rest():
        size = (2, 2, rows, Z, lax.axis_size("w"), 2, lax.axis_size("r"), unit)
        both = shares.reshape(GROUP, rows, part // TILE, 2, TILE)
        return [
            both[:, :, :, at].reshape(size).transpose(2, 3, 4, 5, 0, 6, 1, 7).reshape(rows, GROUP * part).astype(f32)
            for at in range(2)
        ]

    def kernel(ref, gate_ref, up_ref):
        for place, here, there in unit_chunks(unit):
            gate_ref[:, there : there + unit] = ref[place, :, here : here + unit].astype(f32)
            up_ref[:, there : there + unit] = ref[place, :, here + TILE : here + TILE + unit].astype(f32)

    whole = jax.ShapeDtypeStruct((rows, GROUP * part), f32)
    return pl.pallas_call(kernel, out_shape=[whole, whole], name="unpack_units")(shares)


def triangle(length):
    rows = lax.broadcasted_iota(jnp.int32, (length, length), 0)
    cols = lax.broadcasted_iota(jnp.int32, (length, length), 1)
    return rows >= cols


def decays(forget_pre, tri):
    log_gate = jax.nn.log_sigmoid(forget_pre)
    highest = lax.Precision.HIGHEST
    down = jnp.dot(tri, log_gate, preferred_element_type=f32, precision=highest)
    across = lax.dot_general(
        log_gate, tri, (((0,), (1,)), ((), ())), preferred_element_type=f32, precision=highest
    )
    return down, across


def half_mask(half):
    lane = lax.broadcasted_iota(jnp.int32, (1, LANES), 1)
    return (lane >= HEAD) == bool(half)


def attend_kernel(q_ref, k_ref, v_ref, gate_ref, forget_ref, seg_col, seg_row, gated_ref, attended_ref, log_ref):
    length = q_ref.shape[0]
    causal = triangle(length)
    down, across = decays(forget_ref[...], causal.astype(f32))
    bias = jnp.where(causal & (seg_col[...] == seg_row[0]), 0.0, negative_big)
    lane = lax.broadcasted_iota(jnp.int32, (length, LANES), 1)
    logs = jnp.zeros((length, LANES), f32)
    for pair in range(LOCAL_HEADS // 2):
        cols = slice(pair * LANES, (pair + 1) * LANES)
        query, key, value = q_ref[:, cols], k_ref[:, cols], v_ref[:, cols].astype(bf16)
        both = []
        for half in range(2):
            head = 2 * pair + half
            mine = half_mask(half)
            scaled = jnp.where(mine, query, 0) * jnp.asarray(0.125, bf16)
            scores = product_nt(scaled, key) + down[:, head : head + 1] - across[head : head + 1, :] + bias
            top = jnp.max(scores, -1, keepdims=True)
            shifted = jnp.exp(scores - top)
            total = jnp.sum(shifted, -1, keepdims=True)
            probs = (shifted * (1.0 / total)).astype(bf16)
            both.append(jnp.where(mine, product(probs, value), 0.0))
            logs = jnp.where(lane == head, top + jnp.log(total), logs)
        attended = both[0] + both[1]
        attended_ref[:, cols] = attended
        gated_ref[:, cols] = (attended * jax.nn.sigmoid(gate_ref[:, cols])).astype(bf16)
    log_ref[...] = logs


def attend_back_kernel(
    q_ref, k_ref, v_ref, gate_ref, forget_ref, seg_col, seg_row, attended_ref, log_ref, grad_ref, heads_ref, dforget_ref,
):
    length, width = q_ref.shape
    causal = triangle(length)
    tri = causal.astype(f32)
    down, across = decays(forget_ref[...], tri)
    bias = jnp.where(causal & (seg_col[...] == seg_row[0]), 0.0, negative_big)
    lane = lax.broadcasted_iota(jnp.int32, (length, LANES), 1)
    grad_decay = jnp.zeros((length, LANES), f32)
    for pair in range(LOCAL_HEADS // 2):
        cols = slice(pair * LANES, (pair + 1) * LANES)
        query, key, value = q_ref[:, cols], k_ref[:, cols], v_ref[:, cols].astype(bf16)
        out_gate = jax.nn.sigmoid(gate_ref[:, cols])
        grad_gated = grad_ref[:, cols]
        grad_att = (grad_gated * out_gate).astype(bf16)
        grad_gate = (grad_gated * attended_ref[:, cols] * out_gate * (1.0 - out_gate)).astype(bf16)
        dq, dk, dv = [], [], []
        for half in range(2):
            head = 2 * pair + half
            mine = half_mask(half)
            scaled = jnp.where(mine, query, 0) * jnp.asarray(0.125, bf16)
            scores = product_nt(scaled, key) + down[:, head : head + 1] - across[head : head + 1, :] + bias
            probs = jnp.exp(scores - log_ref[:, head : head + 1])
            grad_prob = product_nt(jnp.where(mine, grad_att, 0), value)
            delta = jnp.sum(probs * grad_prob, -1, keepdims=True)
            grad_scores = (probs * (grad_prob - delta)).astype(bf16)
            dq.append(product(grad_scores, key))
            dk.append(product_tn(grad_scores, query))
            dv.append(product_tn(probs.astype(bf16), grad_att))
            one = (lane == head).astype(bf16)
            grad_decay = grad_decay + product(grad_scores, one) - product_tn(grad_scores, one)
        first = half_mask(0)
        found = (
            (jnp.where(first, dq[0], dq[1]) * 0.125).astype(bf16),
            (jnp.where(first, dk[0], dk[1]) * 0.125).astype(bf16),
            jnp.where(first, dv[0], dv[1]).astype(bf16),
            grad_gate,
        )
        for at, one in enumerate(found):
            heads_ref[:, at * width + pair * LANES : at * width + (pair + 1) * LANES] = one
    later = product_tn(tri, grad_decay, lax.Precision.HIGHEST)
    dforget_ref[...] = (later * jax.nn.sigmoid(-forget_ref[...])).astype(bf16)


def attention_specs(length, width, first):
    def columns(at):
        return pl.BlockSpec((length, width), lambda i: (first + i, at))

    lanes = pl.BlockSpec((length, LANES), lambda i: (first + i, 0))
    seg_col = pl.BlockSpec((length, 1), lambda i: (first + i, 0))
    seg_row = pl.BlockSpec((1, 1, length), lambda i: (first + i, 0, 0))
    return columns, lanes, seg_col, seg_row


def attend(query_key, value_gate, forget_pre, seg_col, seg_row, length):
    tokens, width = query_key.shape[0], query_key.shape[1] // 2
    columns, lanes, col_spec, row_spec = attention_specs(length, width, 0)
    return pl.pallas_call(
        attend_kernel,
        grid=(tokens // length,),
        in_specs=[columns(0), columns(1), columns(0), columns(1), lanes, col_spec, row_spec],
        out_specs=[columns(0), columns(0), lanes],
        out_shape=[
            jax.ShapeDtypeStruct((tokens, width), bf16),
            jax.ShapeDtypeStruct((tokens, width), f32),
            jax.ShapeDtypeStruct((tokens, LANES), f32),
        ],
        compiler_params=kernel_params,
        cost_estimate=pl.CostEstimate(
            flops=4 * tokens * length * width, bytes_accessed=14 * tokens * width, transcendentals=0
        ),
        name="attend",
    )(query_key, query_key, value_gate, value_gate, forget_pre, seg_col, seg_row)


def attend_back(query_key, value_gate, forget_pre, seg_col, seg_row, attended, logs, grad_gated, length, first):
    tokens, width = grad_gated.shape
    columns, lanes, col_spec, row_spec = attention_specs(length, width, first)
    own_columns, own_lanes, _, _ = attention_specs(length, width, 0)
    return pl.pallas_call(
        attend_back_kernel,
        grid=(tokens // length,),
        in_specs=[
            columns(0), columns(1), columns(0), columns(1), lanes, col_spec, row_spec,
            columns(0), lanes, own_columns(0),
        ],
        out_specs=[pl.BlockSpec((length, 4 * width), lambda i: (i, 0)), own_lanes],
        out_shape=[
            jax.ShapeDtypeStruct((tokens, 4 * width), bf16),
            jax.ShapeDtypeStruct((tokens, LANES), bf16),
        ],
        compiler_params=kernel_params,
        cost_estimate=pl.CostEstimate(
            flops=0, bytes_accessed=0, transcendentals=0
        ),
        name="attend_back",
    )(query_key, query_key, value_gate, value_gate, forget_pre, seg_col, seg_row, attended, logs, grad_gated)


def attn_terms(hidden, grad_heads, gated, grad_branch, down_term, rows):
    unit = down_term.shape[0] // (2 * Z)
    tokens, width = hidden.shape
    part, half = gated.shape[1], tokens // 2

    def both(left_ref, right_refs):
        near = product_tn(left_ref[:half, :], right_refs[0][...])
        return (near + product_tn(left_ref[half:, :], right_refs[1][...])).astype(bf16)

    def kernel(hidden_ref, near_ref, far_ref, gated_ref, branch_near, branch_far, down_ref, out_ref, out_term):
        at_z = pl.program_id(0)

        @pl.when(at_z == 0)
        def _():
            out_term[...] = both(gated_ref, (branch_near, branch_far))

        term = both(hidden_ref, (near_ref, far_ref))
        for at_y in range(2):
            out_ref[at_y, : 4 * rows] = term[at_y * 4 * rows : (at_y + 1) * 4 * rows]
            first = pl.multiple_of((at_y * 4 + at_z) * rows, rows)
            out_ref[at_y, 4 * rows : 5 * rows] = out_term[pl.ds(first, rows), :]
            out_ref[at_y, 5 * rows :] = down_ref[at_y * unit : (at_y + 1) * unit]

    piece = pl.BlockSpec((half, width), lambda z: (0, 0))
    return pl.pallas_call(
        kernel,
        grid=(Z,),
        in_specs=[
            pl.BlockSpec((tokens, 8 * rows), lambda z: (0, z)),
            piece,
            piece,
            pl.BlockSpec((tokens, part), lambda z: (0, 0)),
            piece,
            piece,
            pl.BlockSpec((2 * unit, width), lambda z: (z, 0)),
        ],
        out_specs=pl.BlockSpec((2, 5 * rows + unit, width), lambda z: (z, 0, 0)),
        out_shape=jax.ShapeDtypeStruct((2 * Z, 5 * rows + unit, width), bf16),
        scratch_shapes=[pltpu.VMEM((part, width), bf16)],
        compiler_params=kernel_params,
        cost_estimate=pl.CostEstimate(
            flops=2 * tokens * width * (width + part), bytes_accessed=10 * tokens * width, transcendentals=0
        ),
        name="attn_terms",
    )(hidden, *grad_heads, gated, *grad_branch, down_term)


def back_through_heads(grad_heads, grad_forget, weight_heads, forget_weight):
    tokens, width = grad_heads.shape
    tile, rows = width // 4, tokens // GROUP

    def kernel(heads_ref, forget_ref, weight_ref, forget_weight_ref, *outs):
        total = product_nt(heads_ref[...], weight_ref[...]) + product_nt(forget_ref[...], forget_weight_ref[...])
        for at, out in enumerate(outs):
            out[...] = total[at * rows : (at + 1) * rows].astype(bf16)

    return pl.pallas_call(
        kernel,
        grid=(4,),
        in_specs=[
            pl.BlockSpec((tokens, width), lambda j: (0, 0)),
            pl.BlockSpec((tokens, LANES), lambda j: (0, 0)),
            pl.BlockSpec((tile, width), lambda j: (j, 0)),
            pl.BlockSpec((tile, LANES), lambda j: (j, 0)),
        ],
        out_specs=[pl.BlockSpec((rows, tile), lambda j: (0, j))] * GROUP,
        out_shape=[jax.ShapeDtypeStruct((rows, width), bf16)] * GROUP,
        compiler_params=kernel_params,
        cost_estimate=pl.CostEstimate(
            flops=2 * tokens * width * width, bytes_accessed=8 * tokens * width, transcendentals=0
        ),
        name="back_through_heads",
    )(grad_heads, grad_forget, weight_heads, forget_weight)


def ffn_tile(hidden_ref, out_grad_ref, both_ref, down_ref, act_ref, dboth_ref, term_ref):
    both = product(hidden_ref[...], both_ref[...])
    gate_ffn, up_ffn = both[:, :TILE], both[:, TILE:]
    grad_act = product_nt(out_grad_ref[...], down_ref[...])
    sigmoid_gate = jax.nn.sigmoid(gate_ffn)
    silu = gate_ffn * sigmoid_gate
    act_ref[...] = (silu * up_ffn).astype(bf16)
    grad_gate = grad_act * up_ffn * sigmoid_gate * (1.0 + gate_ffn * (1.0 - sigmoid_gate))
    dboth_ref[:, :TILE] = grad_gate.astype(bf16)
    dboth_ref[:, TILE:] = (grad_act * silu).astype(bf16)
    term_ref[...] = product_tn(hidden_ref[...], dboth_ref[...]).astype(bf16)


def feed_forward(parts, out_grad, weight_both, weight_down):
    tokens, width = out_grad.shape
    units = weight_down.shape[0]
    steps = units // TILE
    whole = pl.BlockSpec((tokens, width), lambda j: (0, 0))
    rows = tokens // GROUP

    def kernel(*refs):
        joined = refs[GROUP + 3]

        @pl.when(pl.program_id(0) == 0)
        def _():
            for at in range(GROUP):
                joined[at * rows : (at + 1) * rows, :] = refs[at][...]

        ffn_tile(joined, *refs[GROUP : GROUP + 3], *refs[GROUP + 4 :])

    first = pl.BlockSpec((rows, width), lambda j: (0, 0))
    return pl.pallas_call(
        kernel,
        grid=(steps,),
        in_specs=[first] * GROUP
        + [
            whole,
            pl.BlockSpec((width, 2 * TILE), lambda j: (0, j)),
            pl.BlockSpec((TILE, width), lambda j: (j, 0)),
        ],
        out_specs=[
            whole,
            pl.BlockSpec((tokens, TILE), lambda j: (0, j)),
            pl.BlockSpec((tokens, 2 * TILE), lambda j: (0, j)),
            pl.BlockSpec((width, 2 * TILE), lambda j: (0, j)),
        ],
        out_shape=[
            jax.ShapeDtypeStruct((tokens, width), bf16),
            jax.ShapeDtypeStruct((tokens, units), bf16),
            jax.ShapeDtypeStruct((tokens, 2 * units), bf16),
            jax.ShapeDtypeStruct((width, 2 * units), bf16),
        ],
        compiler_params=kernel_params,
        cost_estimate=pl.CostEstimate(
            flops=6 * tokens * width * units, bytes_accessed=12 * tokens * width, transcendentals=0
        ),
        name="feed_forward",
    )(*parts, out_grad, weight_both, weight_down)


def shards(
    inputs,
    segment_ids,
    norm_one,
    w_query,
    w_key,
    w_value,
    w_gate_out,
    w_forget,
    forget_bias,
    w_output,
    norm_two,
    w_ffn_gate,
    w_ffn_up,
    w_ffn_down,
    out_grad,
):
    length, width = inputs.shape
    rows, unit = norm_one.shape[0], w_ffn_down.shape[0]
    size_w, size_r = lax.axis_size("w"), lax.axis_size("r")
    devices = math.prod(lax.axis_size(axis) for axis in ALL)
    place = lax.axis_index("c") * 2 + lax.axis_index("x")
    part = width // GROUP
    units = w_ffn_gate.shape[1] // GROUP
    far = 2 * length
    alone = not has_rest()

    heads_block = exchange(pack_heads((w_query, w_key, w_value, w_gate_out)), ("c", "x"))
    output_block = transpose_quarters(w_output)
    (units_shares,) = order((pack_units(w_ffn_gate, w_ffn_up, unit),), (heads_block,))
    units_block = exchange(units_shares, ("c", "x"))

    attn = [jnp.concatenate((over_rest(heads_block.reshape(4 * rows, width)), over_rest(output_block)), 2)]
    both = [units_block.reshape(4 * rows, 2 * units)]
    if alone:
        down_y = swap(w_ffn_down, "y")
        first = lax.axis_index("y") == 0
        down_pair = jnp.concatenate((jnp.where(first, w_ffn_down, down_y), jnp.where(first, down_y, w_ffn_down)), 0)
    else:
        down_pair = w_ffn_down
    (inputs_sent,) = order((inputs,), (heads_block, down_pair))
    inputs_x = swap(inputs_sent, "x")
    attn_y = [swap(attn[0], "y")]
    attn.append(along_z(attn[0]))

    (attn[1],) = order((attn[1],), (attn_y[0],))
    attn_y.append(swap(attn[1], "y"))
    attn.append(along_z(attn[1]))

    attn[2], out_grad_sent, down_pair = order((attn[2], out_grad, down_pair), (attn_y[1], inputs_x))
    out_grad_x = swap(out_grad_sent, "x")
    attn_y.append(swap(attn[2], "y"))
    attn.append(along_z(attn[2]))

    small = jnp.concatenate(
        (w_forget, norm_one[:, None], norm_two[:, None], jnp.zeros((rows, LANES - H - 2), bf16)), 1
    )
    (small,) = order((small,), (units_block,))
    seg_rows = length // LANES
    seg_own = jnp.pad(segment_ids.astype(bf16).reshape(seg_rows, LANES), ((0, 16 - seg_rows), (0, 0)))
    small = jnp.concatenate((small, seg_own), 0)
    small = exchange(jnp.broadcast_to(small[None], (devices, rows + 16, LANES)), ALL)
    small = small.reshape(devices, rows + 16, LANES)
    members = small[:, rows : rows + seg_rows].reshape(Z, size_w, 2, 2, size_r, 2, seg_rows, LANES)

    def member(other_x, other_c):
        at = [lax.axis_index(axis) for axis in ALL]
        at[5], at[3] = at[5] ^ other_x, at[3] ^ other_c
        return lax.dynamic_slice(members, (*at, 0, 0), (1, 1, 1, 1, 1, 1, seg_rows, LANES)).reshape(1, length)

    seg_all = jnp.concatenate((member(0, 0), member(0, 1), member(1, 0), member(1, 1)), 0).astype(f32)
    seg_col, seg_row = seg_all.reshape(-1, 1), seg_all[:, None, :]
    small = small[:, :rows].reshape(width, LANES)
    gain_one, gain_two = small[:, H].astype(f32), small[:, H + 1].astype(f32)
    forget_weight = lax.dynamic_slice(small, (0, place * LOCAL_HEADS), (width, LOCAL_HEADS))
    forget_weight = jnp.pad(forget_weight, ((0, 0), (0, LANES - LOCAL_HEADS)))
    bias_part = lax.dynamic_slice(forget_bias, (place * LOCAL_HEADS,), (LOCAL_HEADS,)).astype(f32)
    bias_part = jnp.pad(bias_part, (0, LANES - LOCAL_HEADS))

    attn[3], both[0] = order((attn[3], both[0]), (attn_y[2],))
    attn_y.append(swap(attn[3], "y"))
    both.append(along_z(both[0]))
    if alone:
        weight_down = lax.all_gather(down_pair, "z", axis=0, tiled=True)
    else:
        weight_down = gather_units(down_pair.reshape(1, 1, unit, width))

    def attn_order(whole):
        heads = whole[:, :, :, :, : 4 * rows].reshape(Z, 2, size_w, size_r, 2, 2, rows, width)
        out = whole[:, :, :, :, 4 * rows :].reshape(2, 2, 2, size_w, size_r, rows, width)
        return (
            heads.transpose(0, 2, 1, 4, 3, 5, 6, 7).reshape(width, width),
            out.transpose(3, 2, 0, 4, 1, 5, 6).reshape(part, width),
        )

    def attn_spots(outs, at_z, at_y):
        first = pl.multiple_of((at_z * 2 + at_y) * 4 * rows, 4 * rows)
        yield outs[0], 0, 4 * rows, outs[0].at[pl.ds(first, 4 * rows)]
        yield outs[1], 4 * rows, rows, outs[1].at[pl.ds(pl.multiple_of((at_y * 4 + at_z) * rows, rows), rows)]

    arrivals = [(step, other, (attn, attn_y)[other][step]) for step in range(Z) for other in range(2)]
    weight_heads, weight_out = arrange(arrivals, "y", ((width, width), (part, width)), attn_order, attn_spots)

    inputs_all = jnp.concatenate((inputs, swap(inputs, "c"), inputs_x, swap(inputs_x, "c")), 0)
    out_grad_all = jnp.concatenate((out_grad, swap(out_grad, "c"), out_grad_x, swap(out_grad_x, "c")), 0)
    hidden_one = (row_norm(inputs_all.astype(f32))[0] * gain_one).astype(bf16)

    hidden_one, both[0], both[1] = order((hidden_one, both[0], both[1]), (weight_out, out_grad_x))
    both_y = [None] * Z
    both_y[1] = swap(both[1], "y")
    both.append(along_z(both[1]))
    both_y[0] = swap(both[0], "y")
    query_key = product(hidden_one, weight_heads[:, : 2 * part]).astype(bf16)
    value_gate = product(hidden_one, weight_heads[:, 2 * part :])
    forget_pre = product(hidden_one, forget_weight) + bias_part
    gated_att, attended, logs = attend(query_key, value_gate, forget_pre, seg_col, seg_row, length)
    partial = product(gated_att, weight_out).astype(bf16)

    partial, both[2] = order((partial, both[2]), (both_y[1], out_grad_all))
    both_y[2] = swap(both[2], "y")
    both.append(along_z(both[2]))
    branch_x = swap(near_sum(partial[far:]).astype(bf16), "x")
    branch_near = near_sum(partial[:far])

    branch_x, branch_near, both[3] = order((branch_x, branch_near, both[3]), (both_y[0], both_y[2]))
    both_y[3] = swap(both[3], "y")
    tokens = inputs.astype(f32)
    middle = tokens + (branch_near + branch_x.astype(f32))
    normed_two, inv_two = row_norm(middle)
    hidden_own = (normed_two * gain_two).astype(bf16)
    hidden_x = swap(hidden_own, "x")
    hidden_parts = (hidden_own, swap(hidden_own, "c"), hidden_x, swap(hidden_x, "c"))
    if not alone:
        weight_both = gather_units(both[0].reshape(2, 2, rows, 2 * units))
    else:

        def both_spots(outs, at_z, at_y):
            first = pl.multiple_of((at_z * 2 + at_y) * 4 * rows, 4 * rows)
            yield outs[0], 0, 4 * rows, outs[0].at[pl.ds(first, 4 * rows)]

        arrivals = [(step, other, (both, both_y)[other][step]) for step in range(Z) for other in range(2)]
        (weight_both,) = arrange(arrivals, "y", ((width, 2 * units),), None, both_spots)

    hidden_two, activation, grad_both, both_term = feed_forward(hidden_parts, out_grad_all, weight_both, weight_down)
    both_scattered = scatter_units(both_term, 2, rows, ("z", "y"))
    grad_hidden = product_nt(grad_both, weight_both).astype(bf16)
    near_sent = near_sum(grad_hidden[far:]).astype(bf16)
    grad_hidden_x = swap(near_sent, "x")
    near_own = near_sum(grad_hidden[:far])
    (activation,) = order((activation,), (near_sent,))
    down_term = product_tn(activation, out_grad_all).astype(bf16)
    layer_partial = product(activation, weight_down).astype(bf16)
    grad_hidden_x, near_own = order((grad_hidden_x, near_own), (layer_partial, down_term))

    grad_hidden_two = near_own + grad_hidden_x.astype(f32)
    grad_middle = out_grad.astype(f32) + norm_back(grad_hidden_two * gain_two, normed_two, inv_two)
    grad_own = grad_middle.astype(bf16)
    grad_c = swap(grad_own, "c")
    grad_x = swap(grad_own, "x")

    grad_near = jnp.concatenate((grad_own, grad_c), 0)

    def back(grad_branch, first):
        return attend_back(
            query_key, value_gate, forget_pre, seg_col, seg_row,
            attended, logs, product_nt(grad_branch, weight_out), length, first,
        )

    heads_near, forget_near = back(grad_near, 0)
    grad_x, heads_near, layer_partial = order((grad_x, heads_near, layer_partial), ())
    layer_x = swap(near_sum(layer_partial[far:]).astype(bf16), "x")
    layer_near = near_sum(layer_partial[:far])
    grad_far = jnp.concatenate((grad_x, swap(grad_x, "c")), 0)
    heads_far, forget_far = back(grad_far, 2)
    if not alone:
        down_scattered = scatter_units(down_term, 1, unit, ("z",))
    if alone:
        terms = [attn_terms(
            hidden_one, (heads_near, heads_far), gated_att, (grad_near, grad_far), down_term, rows
        )]

        def attn_part(at_z, at_y):
            return lax.dynamic_index_in_dim(terms[-1], at_z * 2 + at_y, 0)[None]

    else:
        grad_heads = jnp.concatenate((heads_near, heads_far), 0)
        grad_branch = jnp.concatenate((grad_near, grad_far), 0)
        heads_term = product_tn(hidden_one, grad_heads).astype(bf16)
        out_term = product_tn(gated_att, grad_branch).astype(bf16)

        def attn_part(at_z, at_y):
            heads = heads_term.reshape(Z, size_w, 2, 2, size_r, 2, rows, width)
            size = (1, size_w, 1, 2, size_r, 2, rows, width)
            heads = lax.dynamic_slice(heads, (at_z, 0, at_y, 0, 0, 0, 0, 0), size)
            heads = heads[0, :, 0].transpose(0, 2, 1, 3, 4, 5).reshape(size_w, size_r, 4 * rows, width)
            out = out_term.reshape(size_w, 2, 2, size_r, 2, rows, width)
            size = (size_w, 1, 1, size_r, 1, rows, width)
            out = lax.dynamic_slice(out, (0, at_y, at_z // 2, 0, at_z % 2, 0, 0), size)
            return jnp.concatenate((heads, out.reshape(size_w, size_r, rows, width)), 2)

    other_y = 1 - lax.axis_index("y")
    attn_sent = attn_part(found_at(1), other_y)
    attn_got = [swap(attn_sent, "y")]
    heads_near, heads_far, forget_near, forget_far = order(
        (heads_near, heads_far, forget_near, forget_far), (attn_sent,)
    )
    if alone:
        terms += order((terms[0],), (attn_sent,))
    grad_forget = jnp.concatenate((forget_near, forget_far), 0)
    forget_term = product_tn(grad_forget, hidden_one)[:8].reshape(8, devices, rows).transpose(1, 0, 2)
    forget_got = exchange(forget_term, ALL)
    bias_sum = jnp.sum(grad_forget.astype(f32), 0)[:LOCAL_HEADS]
    bias_sum = lax.dynamic_update_slice(jnp.zeros((H,), f32), bias_sum, (place * LOCAL_HEADS,))
    attn_later = [attn_part(found_at(step), other_y) for step in range(2, Z + 1)]
    attn_kept = [attn_part(found_at(step), 1 - other_y) for step in range(1, Z + 1)]
    attn_got[0], *attn_later = order((attn_got[0], *attn_later), (forget_term, layer_x))
    attn_total = attn_kept[0].astype(f32) + attn_got[0].astype(f32)
    for step in range(1, Z):
        attn_sent = attn_total.astype(bf16)
        attn_z = along_z(attn_sent)
        if step == 1:
            heads_near, heads_far = order((heads_near, heads_far), (attn_sent,))
            grad_heads = jnp.concatenate((heads_near, heads_far), 0)
            hidden_partial = back_through_heads(grad_heads, grad_forget, weight_heads, forget_weight)
        (sent,) = order((attn_later[step - 1],), (attn_got[step - 1],))
        attn_got.append(swap(sent, "y"))
        if step == 1:
            attn_z, both_scattered, *hidden_partial = order((attn_z, both_scattered, *hidden_partial), (forget_got,))
            hidden_near = core_sum(hidden_partial[0], hidden_partial[1])
            hidden_x = swap(core_sum(hidden_partial[2], hidden_partial[3]).astype(bf16), "x")
            both_block = exchange(both_scattered.reshape(GROUP, rows, 2 * units), ("c", "x"))
            ffn_gate_grad, ffn_up_grad = unpack_units(both_block, unit)
        if step == 2:
            attn_z, hidden_near = order((attn_z, hidden_near), (layer_x,))
            grad_hidden_one = hidden_near + hidden_x.astype(f32)
            normed, inv_one = row_norm(tokens)
            norm_one_partial = jnp.sum(grad_hidden_one * normed, 0)
            norm_two_partial = jnp.sum(grad_hidden_two * normed_two, 0)
            vectors = jnp.concatenate(
                (
                    norm_one_partial.reshape(devices, rows),
                    norm_two_partial.reshape(devices, rows),
                    jnp.broadcast_to(bias_sum[None], (devices, H)),
                ),
                1,
            )
            vectors_got = exchange(vectors, ALL)
            input_grad = grad_middle + norm_back(grad_hidden_one * gain_one, normed, inv_one)
        if step == 3:
            (attn_z,) = order((attn_z,), (vectors_got, ffn_gate_grad))
            layer_output = (middle + (layer_near + layer_x.astype(f32))).astype(bf16)
        attn_total = attn_kept[step].astype(f32) + attn_got[step].astype(f32) + attn_z.astype(f32)
    forget_got = forget_got.reshape(Z * size_w * 2, 2, size_r, 2, 8, rows).sum((0, 2))
    forget_grad = forget_got[:, :, :LOCAL_HEADS].reshape(H, rows).T
    vectors_sum = jnp.sum(vectors_got, 0)
    norm_one_grad, norm_two_grad = vectors_sum[:rows], vectors_sum[rows : 2 * rows]
    forget_bias_grad = vectors_sum[2 * rows :]
    if alone:
        ffn_down_grad = attn_total[0, 0, 5 * rows :]
        attn_sum = attn_total[0, 0, : 5 * rows].astype(bf16)
    else:
        ffn_down_grad = down_scattered.astype(f32)
        attn_sum = sum_over_rest(attn_total).astype(bf16)
    w_output_grad = transpose_quarters(attn_sum[4 * rows :]).astype(f32)
    query_grad, key_grad, value_grad, gate_out_grad = unpack_heads(
        exchange(attn_sum[: 4 * rows].reshape(4, rows, width), ("c", "x")), 4
    )
    return (
        layer_output,
        input_grad,
        norm_one_grad,
        query_grad,
        key_grad,
        value_grad,
        gate_out_grad,
        forget_grad,
        forget_bias_grad,
        w_output_grad,
        norm_two_grad,
        ffn_gate_grad,
        ffn_up_grad,
        ffn_down_grad,
    )


def solution(mesh):
    fsdp, rep = mesh.shape["fsdp"], mesh.shape["rep"]
    finer = Mesh(mesh.devices.reshape(Z, fsdp // 16, 2, 2, rep // 2, 2), ALL)
    rows, line = P(ALL, None), P(ALL)
    in_specs = (
        rows, rows, line, rows, rows, rows, rows, rows, P(), rows, line, rows, rows, rows, rows,
    )
    out_specs = (
        rows, rows, line, rows, rows, rows, rows, rows, P(), rows, line, rows, rows, rows,
    )
    return jax.shard_map(shards, mesh=finer, in_specs=in_specs, out_specs=out_specs, check_vma=False)
```
